256 devices in a mesh: dp: 4 (over z_lo, core), code: 64 (over x, y, z_hi).
Axes of the slice: x: 4, y: 4, z: 8 (z_hi: 4, z_lo: 2; z = z_hi * 2 + z_lo), core: 2. Of those that a mesh axis runs over, the one named last changes fastest.
Arguments:
- latents: bfloat16 [4096, 256], P(('dp', 'code')), may hold values from -32 to 32
- upstream: bfloat16 [4096, 256], P(('dp', 'code')), may hold values from -6 to 6
- targets: int32 [4096], P(('dp', 'code')), may hold values from 0 to 262143
- codebook: float32 [262144, 256], P('code'), may hold values from -1 to 1
- moment_one: float32 [64, 4096, 256], P('code', 'dp'), may hold values from -4 to 4
- moment_two: float32 [64, 4096, 256], P('code', 'dp'), may hold values from 0.01 to 1
Outputs:
- quantized: bfloat16 [4096, 256], P(('dp', 'code'))
- latent_grad: float32 [4096, 256], P(('dp', 'code'))
- new_codebook: float32 [64, 4096, 256], P('code', 'dp')
- new_moment_one: float32 [64, 4096, 256], P('code', 'dp')
- new_moment_two: float32 [64, 4096, 256], P('code', 'dp')
The draws below stay inside these ranges and needn't reach their ends.
All inputs are finite; a program needn't handle non-finite values.
Results may differ from the reference program's by a relative error of at most 0.004.
Values may be sent and summed in bfloat16 or wider, within the bound.
A program may use at most 64 MiB of HBM per device.

```python
import math
from functools import partial
import jax
import jax.numpy as jnp
from jax import lax

K = 262144
C = 256
ADAM_STEP = 100
ROWS = 4096
N_DP = 4
N_CODE = 64


def codebook_table(key):
    return jax.random.truncated_normal(key, -2.5, 2.5, (K, C), jnp.float32) * C ** (-0.5)


def draw_codebook(key, part):
    code_table = codebook_table(key)
    return code_table


def draw_latents(key, part):
    key = jax.random.fold_in(key, 5)
    normal_rows = jax.random.truncated_normal(key, -6.0, 6.0, (ROWS, C), jnp.float32)
    return normal_rows.astype(jnp.bfloat16)


def with_ends(entries, own_key, least, high):
    shape = entries.shape
    place = [jax.random.randint(jax.random.fold_in(own_key, axis), (), 0, shape[axis]) for axis in range(len(shape))]
    entries = entries.at[tuple(place)].set(least)
    longest = shape.index(max(shape))
    place[longest] = (place[longest] + 1) % shape[longest]
    return entries.at[tuple(place)].set(high)


def block_scale(key, shape, split, smallest, high):
    level, own = 1.0, jax.random.fold_in(key, 6)
    for dim, shards_of in split:
        steps = jnp.exp(jax.random.uniform(jax.random.fold_in(own, dim), (shards_of,), jnp.float32, smallest / len(split), high / len(split)))
        level = level * jnp.repeat(steps, shape[dim] // shards_of).reshape([-1 if axis == dim else 1 for axis in range(len(shape))])
    return level


def normal_values(own_key, shape, width, bound, split=(), dtype=jnp.bfloat16):
    loudness = block_scale(own_key, shape, split, -0.22, 0.18) if split else 1.0
    drawn = jax.random.normal(own_key, shape, jnp.float32) * width * loudness
    return jnp.minimum(jnp.maximum(drawn, -bound), bound).astype(dtype)


def setup_inputs(seed: int = 0) -> dict:
    splits = jax.random.split(jax.random.key(seed), 7)
    latents = draw_latents(jax.random.fold_in(splits[6], 71), 0)
    upstream = normal_values(splits[1], (ROWS, C), 1.0, 6.0, ((0, 256),))
    targets = with_ends(jax.random.randint(splits[2], (ROWS,), 0, K), jax.random.fold_in(splits[2], 1), 0, K - 1).astype(jnp.int32)
    codebook = draw_codebook(jax.random.fold_in(splits[6], 71), 0)
    moment_one = normal_values(splits[4], (N_CODE, K // N_CODE, C), 0.3, 4.0, ((0, 64), (1, 4)), jnp.float32)
    moment_two = jnp.clip(jnp.exp(math.log(1.0) - 4.6051702 * jax.random.uniform(splits[5], (N_CODE, K // N_CODE, C), jnp.float32) ** block_scale(splits[5], (N_CODE, K // N_CODE, C), ((0, 64), (1, 4)), -0.2, 0.2)), 0.01, 1.0)
    return dict(latents=latents, upstream=upstream, targets=targets, codebook=codebook, moment_one=moment_one, moment_two=moment_two)


logit_scale = 4.0
commit_weight = 0.5
learn_rate = 0.001
beta_one = 0.9
beta_two = 0.999
adam_eps = 1e-08

def place_rows(values, slot_ids, segment_count):
    return jax.ops.segment_sum(values, slot_ids, num_segments=segment_count)

def reference(latents, upstream, targets, codebook, moment_one, moment_two):
    row_count = latents.shape[0]
    block_width = min(8192, K)
    codes_bf = codebook.astype(jnp.bfloat16)
    blocks = codes_bf.reshape(K // block_width, block_width, C)
    starts = (jnp.arange(K // block_width) * block_width).astype(jnp.int32)
    stacked = jnp.concatenate([latents, upstream], axis=0)

    def score_pair(code_block):
        joined = jnp.dot(stacked, code_block.T, preferred_element_type=jnp.float32)
        return (logit_scale * joined[:row_count], joined[row_count:])

    def online(carry, code_block):
        peak_old, mass_old, weighted_old = carry
        scores, affinity = score_pair(code_block)
        peak_new = jnp.maximum(peak_old, lax.optimization_barrier(jnp.max(scores, axis=1)))
        fade_factor = jnp.exp(peak_old - peak_new)
        exp_terms = jnp.exp(scores - peak_new[:, None])
        return ((peak_new, mass_old * fade_factor + lax.optimization_barrier(jnp.sum(exp_terms, axis=1)), weighted_old * fade_factor + lax.optimization_barrier(jnp.sum(exp_terms * affinity, axis=1))), None)
    zeros_row = jnp.zeros((row_count,), jnp.float32)
    lowest = jnp.full((row_count,), -jnp.inf, jnp.float32)
    (row_max, total_mass, weighted), unused = lax.scan(online, (lowest, zeros_row, zeros_row), blocks)
    mean_affinity = weighted / total_mass
    group_latents = latents.reshape(N_DP, -1, C).astype(jnp.float32)
    group_upstream = upstream.reshape(N_DP, -1, C).astype(jnp.float32)
    group_targets = targets.reshape(N_DP, -1)

    def backward(soft_grad, inputs):
        code_block, start_code = inputs
        scores, affinity = score_pair(code_block)
        probability = jnp.exp(scores - row_max[:, None]) / total_mass[:, None]
        weights = (logit_scale * probability * (affinity - mean_affinity[:, None])).astype(jnp.bfloat16)
        soft_grad = soft_grad + jnp.dot(weights, code_block, preferred_element_type=jnp.float32)
        group_weights = weights.reshape(N_DP, -1, block_width).astype(jnp.float32)
        spread = jnp.einsum('dri,drc->dic', group_weights, group_latents)
        local_index = (group_targets - start_code).astype(jnp.int32)
        in_block = (local_index >= 0) & (local_index < block_width)
        slot_index = jnp.where(in_block, local_index, 0).astype(jnp.int32)
        masked = jnp.where(in_block[:, :, None], group_upstream, 0.0)
        picked = jax.vmap(partial(place_rows, segment_count=block_width))(masked, slot_index)
        rounded = lax.optimization_barrier((spread + picked).astype(jnp.bfloat16))
        return (soft_grad, lax.optimization_barrier(jnp.sum(rounded.astype(jnp.float32), axis=0)))
    soft_grad, grad_blocks = lax.scan(backward, jnp.zeros((row_count, C), jnp.float32), (blocks, starts))
    code_grad = grad_blocks.reshape(K, C)
    quant_rows = codebook[targets]
    quantized = quant_rows.astype(jnp.bfloat16)
    latent_grad = soft_grad + commit_weight * (latents.astype(jnp.float32) - quant_rows)
    fresh_one = beta_one * moment_one.reshape(K, C) + (1.0 - beta_one) * code_grad
    fresh_two = beta_two * moment_two.reshape(K, C) + (1.0 - beta_two) * code_grad * code_grad
    fix_one = 1.0 - beta_one ** ADAM_STEP
    fix_two = 1.0 - beta_two ** ADAM_STEP
    updated = codebook - learn_rate * (fresh_one / fix_one) / (jnp.sqrt(fresh_two / fix_two) + adam_eps)
    out_shape = (N_CODE, K // N_CODE, C)
    return (quantized, latent_grad, updated.reshape(out_shape), fresh_one.reshape(out_shape), fresh_two.reshape(out_shape))
```

```python
import functools

import jax
import jax.numpy as jnp
from jax import lax
from jax.experimental import pallas as pl
from jax.experimental.pallas import tpu as pltpu
from jax.sharding import PartitionSpec as P

ADAM_STEP = 100
logit_scale = 4.0
commit_weight = 0.5
learn_rate = 0.001
beta_one = 0.9
beta_two = 0.999
adam_eps = 1e-08

NX, NY, NZ = 4, 4, 8
MESH = pl.DeviceIdType.MESH
LOG2E = 1.4426950408889634
SCALE = logit_scale * LOG2E
BF = jnp.bfloat16
F32 = jnp.float32


def rows_dot(lhs, rhs):
    return lax.dot_general(lhs, rhs, (((1,), (1,)), ((), ())), preferred_element_type=F32)


def plain_dot(lhs, rhs):
    return jnp.dot(lhs, rhs, preferred_element_type=F32)


def fold_rows(block, op):
    return op(block.reshape(block.shape[0] // 8, 8, block.shape[1]), axis=0)


def merge_stats(parts):
    peak = functools.reduce(jnp.maximum, [part[0] for part in parts])
    fades = [jnp.exp2((part[0] - peak) * SCALE) for part in parts]
    mass = sum(part[1] * fade for part, fade in zip(parts, fades))
    weighted = sum(part[2] * fade for part, fade in zip(parts, fades))
    return peak, mass, weighted


def kernel(
    chunk, stop,
    lat_ref, up_ref, tgt_ref, book_ref,
    quant_ref, grad_ref, code_ref,
    rows, tgt_z, tgt_all, wide, codes, codes_t, expo, aff, weights,
    soft_out, quant_out, rs_one, rs_two, rs_mid, rs_last, rs_three,
    stat_own, stat_x, stat_y, stat_z, stat_mid, stat_fin, code_out, code_in,
    load_sem, gz_s, gz_r, g2_s, g2_r, g3_s, g3_r, tz_s, tz_r, t2_s, t2_r, t3_s, t3_r,
    sx_s, sx_r, sy_s, sy_r, sz_s, sz_r, sf_s, sf_r,
    r1_s, r1_r, r2_s, r2_r, r3_s, r3_r, core_s, core_r,
):
    own_rows, channels = lat_ref.shape
    width = own_rows * NZ
    groups = NX * NY
    blocks = groups // 2
    span = codes.shape[0]
    half = span // 2
    high = NZ // 2
    dp, code = lax.axis_index("dp"), lax.axis_index("code")
    x, y = lax.div(code, NY * high), lax.rem(lax.div(code, high), NY)
    low, core = lax.div(dp, 2), lax.rem(dp, 2)
    z = lax.rem(code, high) * 2 + low

    def at_x(k):
        return lax.rem(x + k, NX)

    def at_y(k):
        return lax.rem(y + k, NY)

    def at_z(k):
        return lax.rem(z + k, NZ)

    def device(px, py, pz, pc):
        return (lax.rem(pz, 2) * 2 + pc, (px * NY + py) * high + lax.div(pz, 2))

    def to_x(k):
        return device(at_x(k), y, z, core)

    def to_y(k):
        return device(x, at_y(k), z, core)

    def to_z(k):
        return device(x, y, at_z(k), core)

    twin = device(x, y, z, 1 - core)
    sent = []

    def push(src, dst, send, recv, target):
        copy = pltpu.make_async_remote_copy(
            src_ref=src, dst_ref=dst, send_sem=send, recv_sem=recv,
            device_id=target, device_id_type=MESH,
        )
        copy.start()
        sent.append(copy)
        return copy

    def arrive(copies):
        for copy in copies:
            copy.wait_recv()

    load = pltpu.make_async_copy(
        book_ref.at[pl.ds(pl.multiple_of(low * span, span), span)], wide, load_sem
    )
    load.start()

    barrier = pltpu.get_barrier_semaphore()
    partners = (
        [to_x(k) for k in range(1, NX)]
        + [to_y(k) for k in range(1, NY)]
        + [to_z(k) for k in range(1, NZ)]
        + [twin]
    )
    for partner in partners:
        pl.semaphore_signal(barrier, inc=1, device_id=partner, device_id_type=MESH)
    pl.semaphore_wait(barrier, len(partners))

    rows[0, x, y, z] = lat_ref[...]
    rows[1, x, y, z] = up_ref[...]
    tgt_z[z] = tgt_ref[...]
    first = [
        push(tgt_z.at[z], tgt_z.at[z], tz_s.at[k], tz_r.at[k], to_z(k)) for k in range(1, NZ)
    ] + [
        push(rows.at[:, x, y, z], rows.at[:, x, y, z], gz_s.at[k], gz_r.at[k], to_z(k))
        for k in range(1, NZ)
    ]
    load.wait()
    codes[...] = wide[...].astype(BF)
    codes_t[...] = wide[...].T.astype(BF)
    arrive(first)
    tgt_all[x, y] = jnp.sum(tgt_z[...], axis=0)
    second = (
        [push(tgt_all.at[x, y], tgt_all.at[x, y], t2_s.at[k], t2_r.at[k], to_y(k)) for k in range(1, NY)]
        + [push(rows.at[0, x, y], rows.at[0, x, y], g2_s.at[0, k], g2_r.at[0, k], to_y(k)) for k in range(1, NY)]
        + [push(rows.at[1, x, y], rows.at[1, x, y], g2_s.at[1, k], g2_r.at[1, k], to_x(k)) for k in range(1, NX)]
    )
    arrive(second)
    third = (
        [push(tgt_all.at[x], tgt_all.at[x], t3_s.at[k], t3_r.at[k], to_x(k)) for k in range(1, NX)]
        + [push(rows.at[0, x], rows.at[0, x], g3_s.at[0, k], g3_r.at[0, k], to_x(k)) for k in range(1, NX)]
        + [push(rows.at[1, :, y], rows.at[1, :, y], g3_s.at[1, k], g3_r.at[1, k], to_y(k)) for k in range(1, NY)]
    )
    arrive(third)

    def place(b):
        return lax.div(b, NY // 2), lax.rem(b, NY // 2) * 2

    def row_block(part, b):
        px, py = place(b)
        return rows[part, px, pl.ds(py, 2)].reshape(2 * width, channels)

    def piece(c):
        return pl.ds(pl.multiple_of(c * chunk, chunk), chunk)

    def finish():
        for copy in sent:
            copy.wait_send()

    def leave():
        quant_ref[...] = rows[0, 0, 0, 0]
        grad_ref[...] = rows[1, 0, 0, 0].astype(F32)
        code_ref[...] = wide[pl.ds(0, half)]
        finish()

    if stop == 1:
        return leave()

    def local_stats(b, carry):
        px, py = place(b)
        lat_b = row_block(0, b)
        up_b = row_block(1, b)

        def scores(c, peak):
            s = rows_dot(codes[piece(c)], lat_b)
            expo[2 * b, piece(c)] = s[:, :width]
            expo[2 * b + 1, piece(c)] = s[:, width:]
            return jnp.maximum(peak, fold_rows(s, jnp.max))

        peak = lax.fori_loop(0, span // chunk, scores, jnp.full((8, 2 * width), -jnp.inf, F32))
        peak = jnp.max(peak, axis=0, keepdims=True)
        shift = peak * SCALE

        def sums(c, carry):
            mass, weighted = carry
            a = rows_dot(codes[piece(c)], up_b)
            s = jnp.concatenate([expo[2 * b, piece(c)], expo[2 * b + 1, piece(c)]], axis=1)
            e = jnp.exp2(s * SCALE - shift)
            expo[2 * b, piece(c)] = e[:, :width]
            expo[2 * b + 1, piece(c)] = e[:, width:]
            aff[2 * b, piece(c)] = a[:, :width]
            aff[2 * b + 1, piece(c)] = a[:, width:]
            return mass + fold_rows(e, jnp.sum), weighted + fold_rows(e * a, jnp.sum)

        zero = jnp.zeros((8, 2 * width), F32)
        mass, weighted = lax.fori_loop(0, span // chunk, sums, (zero, zero))
        mass = jnp.sum(mass, axis=0, keepdims=True)
        weighted = jnp.sum(weighted, axis=0, keepdims=True)
        for k, value in enumerate((peak, mass, weighted)):
            stat_own[px, k, py] = value[:, :width]
            stat_own[px, k, py + 1] = value[:, width:]
        return carry

    lax.fori_loop(0, blocks, local_stats, 0)
    if stop == 2:
        return leave()

    sx = [push(stat_own.at[at_x(k)], stat_x.at[x], sx_s.at[k], sx_r.at[k], to_x(k)) for k in range(1, NX)]

    def back_rows(out):
        def body(b, carry):
            px, py = place(b)
            pair = jnp.concatenate([weights[2 * b], weights[2 * b + 1]], axis=1)
            t = plain_dot(codes_t[...], pair).astype(BF)
            out[px, py] = t[:, :width]
            out[px, py + 1] = t[:, width:]
            return carry

        lax.fori_loop(0, blocks, body, 0)

    def back_codes(part, c):
        total = None
        for b in range(blocks):
            pair = jnp.concatenate([weights[2 * b, piece(c)], weights[2 * b + 1, piece(c)]], axis=1)
            term = plain_dot(pair, row_block(part, b))
            total = term if total is None else total + term
        return total

    base = code * (2 * span) + low * span

    def one_hot(b, carry):
        px, py = place(b)

        def body(c, carry):
            index = lax.broadcasted_iota(jnp.int32, (chunk, width), 0) + (base + c * chunk)
            for side in range(2):
                hit = index == tgt_all[px, py + side]
                weights[2 * b + side, piece(c)] = jnp.where(hit, 1.0, 0.0).astype(BF)
            return carry

        return lax.fori_loop(0, span // chunk, body, carry)

    lax.fori_loop(0, blocks, one_hot, 0)
    back_rows(quant_out)

    def picked(c, carry):
        wide[piece(c)] = back_codes(1, c)
        return carry

    lax.fori_loop(0, span // chunk, picked, 0)

    arrive(sx)
    merged = merge_stats([stat_own[x]] + [stat_x[at_x(k)] for k in range(1, NX)])
    for k in range(3):
        stat_mid[0, k] = merged[k]
    arrive([push(stat_mid.at[0], stat_y.at[y], sy_s.at[k], sy_r.at[k], to_y(k)) for k in range(1, NY)])
    merged = merge_stats([merged] + [stat_y[at_y(k)] for k in range(1, NY)])
    for k in range(3):
        stat_mid[1, k] = merged[k]
    arrive([push(stat_mid.at[1], stat_z.at[z], sz_s.at[k], sz_r.at[k], to_z(k)) for k in range(1, NZ)])
    peak, mass, weighted = merge_stats([merged] + [stat_z[at_z(k)] for k in range(1, NZ)])
    for k, value in enumerate((peak, logit_scale / mass, weighted / mass)):
        stat_fin[x, k] = value
    arrive([push(stat_fin.at[x], stat_fin.at[x], sf_s.at[k], sf_r.at[k], to_x(k)) for k in range(1, NX)])
    if stop == 3:
        return leave()

    def weigh(b, carry):
        px, py = place(b)
        fade = [
            jnp.exp2((stat_own[px, 0, py + side] - stat_fin[px, 0, py + side]) * SCALE)
            * stat_fin[px, 1, py + side]
            for side in range(2)
        ]
        mean = [stat_fin[px, 2, py + side] for side in range(2)]

        def body(c, carry):
            for side in range(2):
                w = expo[2 * b + side, piece(c)] * fade[side]
                w = w * (aff[2 * b + side, piece(c)] - mean[side])
                weights[2 * b + side, piece(c)] = w.astype(BF)
            return carry

        return lax.fori_loop(0, span // chunk, body, carry)

    lax.fori_loop(0, blocks, weigh, 0)
    back_rows(soft_out)

    side_c = channels // 2
    lower, upper = pl.ds(0, side_c), pl.ds(side_c, side_c)
    outs = (soft_out, quant_out)
    one = []
    for n, out in enumerate(outs):
        one += [push(out.at[at_x(k), :, lower], rs_one.at[n, 0, x], r1_s.at[n, 0, k], r1_r.at[n, 0, k], to_x(k)) for k in range(1, NX)]
        one += [push(out.at[:, at_y(k), upper], rs_one.at[n, 1, y], r1_s.at[n, 1, k], r1_r.at[n, 1, k], to_y(k)) for k in range(1, NY)]

    def grad_other(c, carry):
        at = (1 - core) * half + c * chunk
        code_out[piece(c)] = (back_codes_at(at) + wide[pl.ds(pl.multiple_of(at, chunk), chunk)]).astype(BF)
        return carry

    def back_codes_at(at):
        total = None
        where = pl.ds(pl.multiple_of(at, chunk), chunk)
        for b in range(blocks):
            pair = jnp.concatenate([weights[2 * b, where], weights[2 * b + 1, where]], axis=1)
            term = plain_dot(pair, row_block(0, b))
            total = term if total is None else total + term
        return total

    lax.fori_loop(0, half // chunk, grad_other, 0)
    swap = push(code_out, code_in, core_s, core_r, twin)

    def grad_own(c, carry):
        at = core * half + c * chunk
        code_ref[piece(c)] = back_codes_at(at) + wide[pl.ds(pl.multiple_of(at, chunk), chunk)]
        return carry

    lax.fori_loop(0, half // chunk, grad_own, 0)

    arrive(one)
    two = []
    for n, out in enumerate(outs):
        for j in range(NY):
            total = out[x, j, lower].astype(F32)
            for k in range(1, NX):
                total = total + rs_one[n, 0, at_x(k), j].astype(F32)
            rs_mid[n, 0, j] = total.astype(BF)
        for j in range(NX):
            total = out[j, y, upper].astype(F32)
            for k in range(1, NY):
                total = total + rs_one[n, 1, at_y(k), j].astype(F32)
            rs_mid[n, 1, j] = total.astype(BF)
        two += [push(rs_mid.at[n, 0, at_y(k)], rs_two.at[n, 0, y], r2_s.at[n, 0, k], r2_r.at[n, 0, k], to_y(k)) for k in range(1, NY)]
        two += [push(rs_mid.at[n, 1, at_x(k)], rs_two.at[n, 1, x], r2_s.at[n, 1, k], r2_r.at[n, 1, k], to_x(k)) for k in range(1, NX)]
    arrive(two)
    for n in range(2):
        left = rs_mid[n, 0, y].astype(F32)
        for k in range(1, NY):
            left = left + rs_two[n, 0, at_y(k)].astype(F32)
        right = rs_mid[n, 1, x].astype(F32)
        for k in range(1, NX):
            right = right + rs_two[n, 1, at_x(k)].astype(F32)
        total = jnp.concatenate([left, right], axis=0).T.astype(BF)
        rs_last[n] = total.reshape(NZ, own_rows, channels)
    three = [
        push(rs_last.at[:, at_z(k)], rs_three.at[:, z], r3_s.at[k], r3_r.at[k], to_z(k)) for k in range(1, NZ)
    ]
    swap.wait_recv()
    code_ref[...] = code_ref[...] + code_in[...].astype(F32)
    arrive(three)
    soft = rs_last[0, z].astype(F32)
    quant = rs_last[1, z].astype(F32)
    for k in range(1, NZ):
        soft = soft + rs_three[0, at_z(k)].astype(F32)
        quant = quant + rs_three[1, at_z(k)].astype(F32)
    quant_ref[...] = quant.astype(BF)
    grad_ref[...] = soft + commit_weight * (lat_ref[...].astype(F32) - quant)
    finish()


def exchange(latents, upstream, targets, codebook, stop=0):
    own_rows, channels = latents.shape
    width = own_rows * NZ
    span = codebook.shape[0] // 2
    half = span // 2
    groups = NX * NY
    chunk = min(512, half)
    z = lax.rem(lax.axis_index("code"), NZ // 2) * 2 + lax.div(lax.axis_index("dp"), 2)
    spread = jnp.where(jnp.arange(NZ)[:, None] == z, targets[None, :], 0).reshape(1, width)
    dma = pltpu.SemaphoreType.DMA
    side_c = channels // 2
    in_vmem = pl.BlockSpec(memory_space=pltpu.VMEM)
    scratch = [
        pltpu.VMEM((2, NX, NY, NZ, own_rows, channels), BF),
        pltpu.VMEM((NZ, 1, width), jnp.int32),
        pltpu.VMEM((NX, NY, 1, width), jnp.int32),
        pltpu.VMEM((span, channels), F32),
        pltpu.VMEM((span, channels), BF),
        pltpu.VMEM((channels, span), BF),
        pltpu.VMEM((groups, span, width), F32),
        pltpu.VMEM((groups, span, width), F32),
        pltpu.VMEM((groups, span, width), BF),
        pltpu.VMEM((NX, NY, channels, width), BF),
        pltpu.VMEM((NX, NY, channels, width), BF),
        pltpu.VMEM((2, 2, NX, NY, side_c, width), BF),
        pltpu.VMEM((2, 2, NX, side_c, width), BF),
        pltpu.VMEM((2, 2, NX, side_c, width), BF),
        pltpu.VMEM((2, NZ, own_rows, channels), BF),
        pltpu.VMEM((2, NZ, own_rows, channels), BF),
        pltpu.VMEM((NX, 3, NY, 1, width), F32),
        pltpu.VMEM((NX, 3, NY, 1, width), F32),
        pltpu.VMEM((NY, 3, NY, 1, width), F32),
        pltpu.VMEM((NZ, 3, NY, 1, width), F32),
        pltpu.VMEM((2, 3, NY, 1, width), F32),
        pltpu.VMEM((NX, 3, NY, 1, width), F32),
        pltpu.VMEM((half, channels), BF),
        pltpu.VMEM((half, channels), BF),
        dma,
        dma((NZ,)), dma((NZ,)), dma((2, NX)), dma((2, NX)), dma((2, NX)), dma((2, NX)),
        dma((NZ,)), dma((NZ,)), dma((NY,)), dma((NY,)), dma((NX,)), dma((NX,)),
        dma((NX,)), dma((NX,)), dma((NY,)), dma((NY,)), dma((NZ,)), dma((NZ,)), dma((NX,)), dma((NX,)),
        dma((2, 2, NX)), dma((2, 2, NX)), dma((2, 2, NX)), dma((2, 2, NX)), dma((NZ,)), dma((NZ,)),
        dma, dma,
    ]
    return pl.pallas_call(
        functools.partial(kernel, chunk, stop),
        out_shape=(
            jax.ShapeDtypeStruct((own_rows, channels), BF),
            jax.ShapeDtypeStruct((own_rows, channels), F32),
            jax.ShapeDtypeStruct((half, channels), F32),
        ),
        in_specs=[in_vmem, in_vmem, in_vmem, pl.BlockSpec(memory_space=pl.ANY)],
        out_specs=(in_vmem, in_vmem, in_vmem),
        scratch_shapes=scratch,
        compiler_params=pltpu.CompilerParams(
            collective_id=0, has_side_effects=True, vmem_limit_bytes=60 * 1024 * 1024
        ),
    )(latents, upstream, spread, codebook)


def per_device(latents, upstream, targets, codebook, moment_one, moment_two, stop=0):
    quantized, latent_grad, code_grad = exchange(latents, upstream, targets, codebook, stop)
    quarter = code_grad.shape[0]
    own_codes = lax.dynamic_slice_in_dim(codebook, lax.axis_index("dp") * quarter, quarter, 0)
    fresh_one = beta_one * moment_one[0] + (1.0 - beta_one) * code_grad
    fresh_two = beta_two * moment_two[0] + (1.0 - beta_two) * code_grad * code_grad
    fix_one = 1.0 - beta_one**ADAM_STEP
    fix_two = 1.0 - beta_two**ADAM_STEP
    updated = own_codes - learn_rate * (fresh_one / fix_one) / (
        jnp.sqrt(fresh_two / fix_two) + adam_eps
    )
    return (quantized, latent_grad, updated[None], fresh_one[None], fresh_two[None])


def solution(mesh, stop=0):
    return jax.shard_map(
        functools.partial(per_device, stop=stop),
        mesh=mesh,
        in_specs=(
            P(("dp", "code"), None),
            P(("dp", "code"), None),
            P(("dp", "code")),
            P("code", None),
            P("code", "dp", None),
            P("code", "dp", None),
        ),
        out_specs=(
            P(("dp", "code"), None),
            P(("dp", "code"), None),
            P("code", "dp", None),
            P("code", "dp", None),
            P("code", "dp", None),
        ),
        check_vma=False,
    )
```

```python
import functools

import jax
import jax.numpy as jnp
from jax import lax
from jax.experimental import pallas as pl
from jax.experimental.pallas import tpu as pltpu
from jax.sharding import PartitionSpec as P

ADAM_STEP = 100
logit_scale = 4.0
commit_weight = 0.5
learn_rate = 0.001
beta_one = 0.9
beta_two = 0.999
adam_eps = 1e-08

NX, NY, NZ = 4, 4, 8
MESH = pl.DeviceIdType.MESH
LOG2E = 1.4426950408889634
SCALE = logit_scale * LOG2E
BF = jnp.bfloat16
F32 = jnp.float32


def rows_dot(lhs, rhs):
    return lax.dot_general(lhs, rhs, (((1,), (1,)), ((), ())), preferred_element_type=F32)


def plain_dot(lhs, rhs):
    return jnp.dot(lhs, rhs, preferred_element_type=F32)


def fold_rows(block, op):
    return op(block.reshape(block.shape[0] // 16, 16, block.shape[1]), axis=0)


def merge_stats(parts):
    peak = functools.reduce(jnp.maximum, [part[0] for part in parts])
    fades = [jnp.exp2((part[0] - peak) * SCALE) for part in parts]
    mass = sum(part[1] * fade for part, fade in zip(parts, fades))
    weighted = sum(part[2] * fade for part, fade in zip(parts, fades))
    return peak, mass, weighted


def kernel(
    chunk,
    lat_ref, up_ref, tgt_ref, book_ref,
    terms_ref, code_ref,
    rows, tgt_z, tgt_all, wide, codes, codes_t, expo, aff, weights,
    soft_out, quant_out, rs_one, rs_two, rs_mid, rs_last, rs_three,
    stat_own, stat_x, stat_y, stat_z, stat_mid, stat_fin, code_out, code_in,
    load_sem, gz_s, gz_r, g2_s, g2_r, g3_s, g3_r, tz_s, tz_r, t2_s, t2_r, t3_s, t3_r,
    sx_s, sx_r, sy_s, sy_r, sz_s, sz_r, sf_s, sf_r,
    rx_s, rx_r, ry_s, ry_r, r2_s, r2_r, r3_s, r3_r, core_s, core_r,
):
    own_rows, channels = lat_ref.shape
    width = own_rows * NZ
    groups = NX * NY
    blocks = groups // 2
    span = codes.shape[0]
    half = span // 2
    high = NZ // 2
    dp, code = lax.axis_index("dp"), lax.axis_index("code")
    x, y = lax.div(code, NY * high), lax.rem(lax.div(code, high), NY)
    low, core = lax.div(dp, 2), lax.rem(dp, 2)
    z = lax.rem(code, high) * 2 + low

    def at_x(k):
        return lax.rem(x + k, NX)

    def at_y(k):
        return lax.rem(y + k, NY)

    def at_z(k):
        return lax.rem(z + k, NZ)

    def device(px, py, pz, pc):
        return (lax.rem(pz, 2) * 2 + pc, (px * NY + py) * high + lax.div(pz, 2))

    def to_x(k):
        return device(at_x(k), y, z, core)

    def to_y(k):
        return device(x, at_y(k), z, core)

    def to_z(k):
        return device(x, y, at_z(k), core)

    twin = device(x, y, z, 1 - core)
    sent = []

    def push(src, dst, send, recv, target):
        copy = pltpu.make_async_remote_copy(
            src_ref=src, dst_ref=dst, send_sem=send, recv_sem=recv,
            device_id=target, device_id_type=MESH,
        )
        copy.start()
        sent.append(copy)
        return copy

    def arrive(copies):
        for copy in copies:
            copy.wait_recv()

    load = pltpu.make_async_copy(
        book_ref.at[pl.ds(pl.multiple_of(low * span, span), span)], wide, load_sem
    )
    load.start()

    barrier = pltpu.get_barrier_semaphore()
    partners = (
        [to_z(k) for k in range(1, NZ)]
        + [to_x(k) for k in range(1, NX)]
        + [to_y(k) for k in range(1, NY)]
        + [twin]
    )
    for partner in partners:
        pl.semaphore_signal(barrier, inc=1, device_id=partner, device_id_type=MESH)

    rows[0, x, y, z] = lat_ref[...]
    rows[1, x, y, z] = up_ref[...]
    lane = lax.broadcasted_iota(jnp.int32, (1, width), 1) - z * own_rows
    own_targets = jnp.zeros((1, width), jnp.int32)
    for k in range(own_rows):
        own_targets = jnp.where(lane == k, tgt_ref[k], own_targets)
    tgt_z[z] = own_targets
    pl.semaphore_wait(barrier, len(partners))

    far_first = sorted(range(1, NZ), key=lambda k: -min(k, NZ - k))
    first = [
        push(rows.at[:, x, y, z], rows.at[:, x, y, z], gz_s.at[k], gz_r.at[k], to_z(k))
        for k in far_first
    ] + [
        push(tgt_z.at[z], tgt_z.at[z], tz_s.at[k], tz_r.at[k], to_z(k)) for k in far_first
    ]
    load.wait()
    codes[...] = wide[...].astype(BF)
    codes_t[...] = wide[...].T.astype(BF)
    arrive(first)
    tgt_all[x, y] = jnp.sum(tgt_z[...], axis=0)
    second = (
        [push(tgt_all.at[x, y], tgt_all.at[x, y], t2_s.at[k], t2_r.at[k], to_y(k)) for k in range(1, NY)]
        + [push(rows.at[0, x, y], rows.at[0, x, y], g2_s.at[0, k], g2_r.at[0, k], to_y(k)) for k in range(1, NY)]
        + [push(rows.at[1, x, y], rows.at[1, x, y], g2_s.at[1, k], g2_r.at[1, k], to_x(k)) for k in range(1, NX)]
    )
    arrive(second)
    third_tgt = [push(tgt_all.at[x], tgt_all.at[x], t3_s.at[k], t3_r.at[k], to_x(k)) for k in range(1, NX)]
    third_lat, third_up = {}, {}
    for k in (1, NX - 1, 2) if NX > 2 else (1,):
        third_lat[k] = push(rows.at[0, x], rows.at[0, x], g3_s.at[0, k], g3_r.at[0, k], to_x(k))
        third_up[k] = push(rows.at[1, :, y], rows.at[1, :, y], g3_s.at[1, k], g3_r.at[1, k], to_y(k))

    pairs = NY // 2

    def row_block(part, px, py):
        return rows[part, px, pl.ds(py, 2)].reshape(2 * width, channels)

    def piece(c):
        return pl.ds(c * chunk, chunk)

    pieces = span // chunk

    def scores(px):
        def body(j, carry):
            py = j * 2
            g = px * NY + py
            lat_b = row_block(0, px, py)
            peak = jnp.full((16, 2 * width), -jnp.inf, F32)
            for c in range(pieces):
                s = rows_dot(codes[piece(c)], lat_b)
                expo[g, piece(c)] = s[:, :width]
                expo[g + 1, piece(c)] = s[:, width:]
                peak = jnp.maximum(peak, fold_rows(s, jnp.max))
            peak = jnp.max(peak, axis=0, keepdims=True)
            stat_own[px, 0, py] = peak[:, :width]
            stat_own[px, 0, py + 1] = peak[:, width:]
            return carry

        lax.fori_loop(0, pairs, body, 0)

    def sums(b, carry):
        px, py = lax.div(b, pairs), lax.rem(b, pairs) * 2
        up_b = row_block(1, px, py)
        shift = jnp.concatenate([stat_own[px, 0, py], stat_own[px, 0, py + 1]], axis=1) * SCALE
        mass = jnp.zeros((16, 2 * width), F32)
        weighted = jnp.zeros((16, 2 * width), F32)
        for c in range(pieces):
            a = rows_dot(codes[piece(c)], up_b)
            s = jnp.concatenate([expo[2 * b, piece(c)], expo[2 * b + 1, piece(c)]], axis=1)
            e = jnp.exp2(s * SCALE - shift)
            expo[2 * b, piece(c)] = e[:, :width]
            expo[2 * b + 1, piece(c)] = e[:, width:]
            aff[2 * b, piece(c)] = a[:, :width]
            aff[2 * b + 1, piece(c)] = a[:, width:]
            mass = mass + fold_rows(e, jnp.sum)
            weighted = weighted + fold_rows(e * a, jnp.sum)
        mass = jnp.sum(mass, axis=0, keepdims=True)
        weighted = jnp.sum(weighted, axis=0, keepdims=True)
        for k, value in enumerate((mass, weighted)):
            stat_own[px, k + 1, py] = value[:, :width]
            stat_own[px, k + 1, py + 1] = value[:, width:]
        return carry

    def back_rows(out, px, py):
        g = px * NY + py
        pair = jnp.concatenate([weights[g], weights[g + 1]], axis=1)
        t = plain_dot(codes_t[...], pair).astype(BF)
        out[px, py] = t[:, :width]
        out[px, py + 1] = t[:, width:]

    def back_codes(part, at):
        where = pl.ds(pl.multiple_of(at, chunk), chunk)
        total = None
        for b in range(blocks):
            pair = jnp.concatenate([weights[2 * b, where], weights[2 * b + 1, where]], axis=1)
            term = plain_dot(pair, row_block(part, b // pairs, b % pairs * 2))
            total = term if total is None else total + term
        return total

    base = code * (2 * span) + low * span
    index = lax.broadcasted_iota(jnp.int32, (chunk, width), 0)

    def one_hot(b, carry):
        px, py = lax.div(b, pairs), lax.rem(b, pairs) * 2
        for side in range(2):
            local = tgt_all[px, py + side] - base
            for c in range(pieces):
                weights[2 * b + side, piece(c)] = jnp.where(index == local - c * chunk, 1.0, 0.0).astype(BF)
        back_rows(quant_out, px, py)
        return carry

    side_c = channels // 2
    lower, upper = pl.ds(0, side_c), pl.ds(side_c, side_c)

    def send_plane(n, out, k):
        px = at_x(k)
        copies = []
        if k:
            copies.append(push(out.at[px, :, lower], rs_one.at[n, 0, x], rx_s.at[n, k], rx_r.at[n, k], to_x(k)))
        for j in range(1, NY):
            copies.append(
                push(out.at[px, at_y(j), upper], rs_one.at[n, 1, y, px], ry_s.at[n, k, j], ry_r.at[n, k, j], to_y(j))
            )
        return copies

    def reduce_one(n, out):
        for j in range(NY):
            total = out[x, j, lower].astype(F32)
            for k in range(1, NX):
                total = total + rs_one[n, 0, at_x(k), j].astype(F32)
            rs_mid[n, 0, j] = total.astype(BF)
        copies = [
            push(rs_mid.at[n, 0, at_y(k)], rs_two.at[n, 0, y], r2_s.at[n, 0, k], r2_r.at[n, 0, k], to_y(k))
            for k in range(1, NY)
        ]
        for j in range(NX):
            total = out[j, y, upper].astype(F32)
            for k in range(1, NY):
                total = total + rs_one[n, 1, at_y(k), j].astype(F32)
            rs_mid[n, 1, j] = total.astype(BF)
        return copies + [
            push(rs_mid.at[n, 1, at_x(k)], rs_two.at[n, 1, x], r2_s.at[n, 1, k], r2_r.at[n, 1, k], to_x(k))
            for k in range(1, NX)
        ]

    def reduce_two(n):
        left = rs_mid[n, 0, y].astype(F32)
        for k in range(1, NY):
            left = left + rs_two[n, 0, at_y(k)].astype(F32)
        right = rs_mid[n, 1, x].astype(F32)
        for k in range(1, NX):
            right = right + rs_two[n, 1, at_x(k)].astype(F32)
        total = jnp.concatenate([left, right], axis=0).T.astype(BF)
        rs_last[n] = total.reshape(NZ, own_rows, channels)
        return [
            push(rs_last.at[n, at_z(k)], rs_three.at[n, z], r3_s.at[n, k], r3_r.at[n, k], to_z(k))
            for k in far_first
        ]

    def reduce_three(n):
        total = rs_last[n, z].astype(F32)
        for k in range(1, NZ):
            total = total + rs_three[n, at_z(k)].astype(F32)
        return total

    arrive(third_tgt)
    lax.fori_loop(0, blocks, one_hot, 0)
    scores(x)
    for k in third_lat:
        arrive([third_lat[k]])
        scores(at_x(NX - k))
    arrive(third_up.values())
    quant_one = []
    for k in (2, 1, 3, 0) if NX > 2 else (1, 0):
        quant_one += send_plane(1, quant_out, k)
    lax.fori_loop(0, blocks, sums, 0)

    sx = [push(stat_own.at[at_x(k)], stat_x.at[x], sx_s.at[k], sx_r.at[k], to_x(k)) for k in range(1, NX)]

    def picked(c, carry):
        at = c * chunk
        wide[pl.ds(pl.multiple_of(at, chunk), chunk)] = back_codes(1, at)
        return carry

    lax.fori_loop(0, pieces, picked, 0)
    arrive(sx)
    merged = merge_stats([stat_own[x]] + [stat_x[at_x(k)] for k in range(1, NX)])
    for k in range(3):
        stat_mid[0, k] = merged[k]
    sy = [push(stat_mid.at[0], stat_y.at[y], sy_s.at[k], sy_r.at[k], to_y(k)) for k in range(1, NY)]
    arrive(quant_one)
    quant_two = reduce_one(1, quant_out)
    arrive(sy)
    merged = merge_stats([merged] + [stat_y[at_y(k)] for k in range(1, NY)])
    for k in range(3):
        stat_mid[1, k] = merged[k]
    sz = [push(stat_mid.at[1], stat_z.at[z], sz_s.at[k], sz_r.at[k], to_z(k)) for k in far_first]
    arrive(quant_two)
    quant_three = reduce_two(1)
    arrive(sz)
    peak, mass, weighted = merge_stats([merged] + [stat_z[at_z(k)] for k in range(1, NZ)])
    for k, value in enumerate((peak, logit_scale / mass, weighted / mass)):
        stat_fin[x, k] = value
    arrive([push(stat_fin.at[x], stat_fin.at[x], sf_s.at[k], sf_r.at[k], to_x(k)) for k in range(1, NX)])

    def weigh(px):
        def body(j, carry):
            py = j * 2
            g = px * NY + py
            for side in range(2):
                fade = (
                    jnp.exp2((stat_own[px, 0, py + side] - stat_fin[px, 0, py + side]) * SCALE)
                    * stat_fin[px, 1, py + side]
                )
                mean = stat_fin[px, 2, py + side]
                for c in range(pieces):
                    w = expo[g + side, piece(c)] * fade * (aff[g + side, piece(c)] - mean)
                    weights[g + side, piece(c)] = w.astype(BF)
            back_rows(soft_out, px, py)
            return carry

        lax.fori_loop(0, pairs, body, 0)

    soft_one = []
    for k in (2, 1, 3, 0) if NX > 2 else (1, 0):
        weigh(at_x(k))
        soft_one += send_plane(0, soft_out, k)

    def grad_other(c, carry):
        at = (1 - core) * half + c * chunk
        where = pl.ds(pl.multiple_of(at, chunk), chunk)
        code_out[pl.ds(pl.multiple_of(c * chunk, chunk), chunk)] = (back_codes(0, at) + wide[where]).astype(BF)
        return carry

    lax.fori_loop(0, half // chunk, grad_other, 0)
    swap = push(code_out, code_in, core_s, core_r, twin)
    arrive(soft_one)
    soft_two = reduce_one(0, soft_out)

    def grad_own(c, carry):
        at = core * half + c * chunk
        where = pl.ds(pl.multiple_of(at, chunk), chunk)
        code_ref[pl.ds(pl.multiple_of(c * chunk, chunk), chunk)] = back_codes(0, at) + wide[where]
        return carry

    lax.fori_loop(0, half // chunk, grad_own, 0)
    arrive(soft_two)
    soft_three = reduce_two(0)
    swap.wait_recv()
    code_ref[...] = code_ref[...] + code_in[...].astype(F32)
    arrive(quant_three)
    terms_ref[1] = reduce_three(1)
    arrive(soft_three)
    terms_ref[0] = reduce_three(0)
    for copy in sent:
        copy.wait_send()


def exchange(latents, upstream, targets, codebook):
    own_rows, channels = latents.shape
    width = own_rows * NZ
    span = codebook.shape[0] // 2
    half = span // 2
    groups = NX * NY
    chunk = min(256, half)
    dma = pltpu.SemaphoreType.DMA
    side_c = channels // 2
    in_vmem = pl.BlockSpec(memory_space=pltpu.VMEM)
    scratch = [
        pltpu.VMEM((2, NX, NY, NZ, own_rows, channels), BF),
        pltpu.VMEM((NZ, 1, width), jnp.int32),
        pltpu.VMEM((NX, NY, 1, width), jnp.int32),
        pltpu.VMEM((span, channels), F32),
        pltpu.VMEM((span, channels), BF),
        pltpu.VMEM((channels, span), BF),
        pltpu.VMEM((groups, span, width), F32),
        pltpu.VMEM((groups, span, width), F32),
        pltpu.VMEM((groups, span, width), BF),
        pltpu.VMEM((NX, NY, channels, width), BF),
        pltpu.VMEM((NX, NY, channels, width), BF),
        pltpu.VMEM((2, 2, NX, NY, side_c, width), BF),
        pltpu.VMEM((2, 2, NX, side_c, width), BF),
        pltpu.VMEM((2, 2, NX, side_c, width), BF),
        pltpu.VMEM((2, NZ, own_rows, channels), BF),
        pltpu.VMEM((2, NZ, own_rows, channels), BF),
        pltpu.VMEM((NX, 3, NY, 1, width), F32),
        pltpu.VMEM((NX, 3, NY, 1, width), F32),
        pltpu.VMEM((NY, 3, NY, 1, width), F32),
        pltpu.VMEM((NZ, 3, NY, 1, width), F32),
        pltpu.VMEM((2, 3, NY, 1, width), F32),
        pltpu.VMEM((NX, 3, NY, 1, width), F32),
        pltpu.VMEM((half, channels), BF),
        pltpu.VMEM((half, channels), BF),
        dma,
        dma((NZ,)), dma((NZ,)), dma((2, NX)), dma((2, NX)), dma((2, NX)), dma((2, NX)),
        dma((NZ,)), dma((NZ,)), dma((NY,)), dma((NY,)), dma((NX,)), dma((NX,)),
        dma((NX,)), dma((NX,)), dma((NY,)), dma((NY,)), dma((NZ,)), dma((NZ,)), dma((NX,)), dma((NX,)),
        dma((2, NX)), dma((2, NX)), dma((2, NX, NY)), dma((2, NX, NY)),
        dma((2, 2, NX)), dma((2, 2, NX)), dma((2, NZ)), dma((2, NZ)),
        dma, dma,
    ]
    return pl.pallas_call(
        functools.partial(kernel, chunk),
        out_shape=(
            jax.ShapeDtypeStruct((2, own_rows, channels), F32),
            jax.ShapeDtypeStruct((half, channels), F32),
        ),
        in_specs=[in_vmem, in_vmem, pl.BlockSpec(memory_space=pltpu.SMEM), pl.BlockSpec(memory_space=pl.ANY)],
        out_specs=(in_vmem, in_vmem),
        scratch_shapes=scratch,
        compiler_params=pltpu.CompilerParams(
            collective_id=0, has_side_effects=True, vmem_limit_bytes=60 * 1024 * 1024
        ),
    )(latents, upstream, targets, codebook)


def finish(terms, lat, grad, book, one, two, quant_ref, lat_ref, book_ref, one_ref, two_ref, held, sem_in, sem_out):
    quarter = grad.shape[0]
    steps = 4
    size = quarter // steps
    own = lax.axis_index("dp") * quarter
    sources = (grad, book, one.at[0], two.at[0])
    targets = (book_ref.at[0], one_ref.at[0], two_ref.at[0])
    fix_one = 1.0 - beta_one**ADAM_STEP
    fix_two = 1.0 - beta_two**ADAM_STEP

    def fetch(n, c):
        start = own + c * size if n == 1 else c * size
        where = pl.ds(pl.multiple_of(start, size), size)
        return pltpu.make_async_copy(sources[n].at[where], held.at[n, pl.ds(c * size, size)], sem_in.at[n, c])

    def put(n, c):
        where = pl.ds(c * size, size)
        return pltpu.make_async_copy(held.at[4 + n, where], targets[n].at[where], sem_out.at[n, c])

    for c in range(steps):
        for n in range(4):
            fetch(n, c).start()
    quant = terms[1]
    quant_ref[...] = quant.astype(BF)
    lat_ref[...] = terms[0] + commit_weight * (lat[...].astype(F32) - quant)
    for c in range(steps):
        for n in range(4):
            fetch(n, c).wait()
        where = pl.ds(c * size, size)
        slope = held[0, where]
        fresh_one = beta_one * held[2, where] + (1.0 - beta_one) * slope
        fresh_two = beta_two * held[3, where] + (1.0 - beta_two) * slope * slope
        held[5, where] = fresh_one
        held[6, where] = fresh_two
        held[4, where] = held[1, where] - learn_rate * (fresh_one / fix_one) / (
            jnp.sqrt(fresh_two / fix_two) + adam_eps
        )
        for n in range(3):
            put(n, c).start()
    for c in range(steps):
        for n in range(3):
            put(n, c).wait()


def per_device(latents, upstream, targets, codebook, moment_one, moment_two):
    terms, code_grad = exchange(latents, upstream, targets, codebook)
    quarter, channels = code_grad.shape
    in_vmem = pl.BlockSpec(memory_space=pltpu.VMEM)
    anywhere = pl.BlockSpec(memory_space=pl.ANY)
    moment = jax.ShapeDtypeStruct(moment_one.shape, F32)
    return pl.pallas_call(
        finish,
        out_shape=(
            jax.ShapeDtypeStruct(latents.shape, BF),
            jax.ShapeDtypeStruct(latents.shape, F32),
            moment, moment, moment,
        ),
        in_specs=[in_vmem, in_vmem, anywhere, anywhere, anywhere, anywhere],
        out_specs=(in_vmem, in_vmem, anywhere, anywhere, anywhere),
        scratch_shapes=[
            pltpu.VMEM((7, quarter, channels), F32),
            pltpu.SemaphoreType.DMA((4, 4)),
            pltpu.SemaphoreType.DMA((3, 4)),
        ],
        compiler_params=pltpu.CompilerParams(vmem_limit_bytes=60 * 1024 * 1024),
    )(terms, latents, code_grad, codebook, moment_one, moment_two)


def solution(mesh):
    return jax.shard_map(
        per_device,
        mesh=mesh,
        in_specs=(
            P(("dp", "code"), None),
            P(("dp", "code"), None),
            P(("dp", "code")),
            P("code", None),
            P("code", "dp", None),
            P("code", "dp", None),
        ),
        out_specs=(
            P(("dp", "code"), None),
            P(("dp", "code"), None),
            P("code", "dp", None),
            P("code", "dp", None),
            P("code", "dp", None),
        ),
        check_vma=False,
    )
```

```python
import functools

import jax
import jax.numpy as jnp
from jax import lax
from jax.experimental import pallas as pl
from jax.experimental.pallas import tpu as pltpu
from jax.sharding import PartitionSpec as P

ADAM_STEP = 100
logit_scale = 4.0
commit_weight = 0.5
learn_rate = 0.001
beta_one = 0.9
beta_two = 0.999
adam_eps = 1e-08

NX, NY, NZ = 4, 4, 8
MESH = pl.DeviceIdType.MESH
LOG2E = 1.4426950408889634
SCALE = logit_scale * LOG2E
BF = jnp.bfloat16
F32 = jnp.float32


def rows_dot(lhs, rhs):
    return lax.dot_general(lhs, rhs, (((1,), (1,)), ((), ())), preferred_element_type=F32)


def plain_dot(lhs, rhs):
    return jnp.dot(lhs, rhs, preferred_element_type=F32)


def fold_rows(block, op):
    return op(block.reshape(block.shape[0] // 16, 16, block.shape[1]), axis=0)


def merge_stats(parts):
    peak = functools.reduce(jnp.maximum, [part[0] for part in parts])
    fades = [jnp.exp2((part[0] - peak) * SCALE) for part in parts]
    mass = sum(part[1] * fade for part, fade in zip(parts, fades))
    weighted = sum(part[2] * fade for part, fade in zip(parts, fades))
    return peak, mass, weighted


def kernel(
    chunk,
    lat_ref, up_ref, tgt_ref, book_ref, one_ref, two_ref,
    terms_ref, adam,
    rows, tgt_z, tgt_all, wide, codes, codes_t, expo, aff, weights,
    soft_out, quant_out, rs_one, rs_two, rs_mid, rs_last, rs_three,
    stat_own, stat_x, stat_y, stat_z, stat_mid, stat_fin, code_out, code_in, own_grad,
    load_sem, adam_s, gz_s, gz_r, g2_s, g2_r, gx_s, gx_r, tz_s, tz_r, t2_s, t2_r, t3_s, t3_r,
    sx_s, sx_r, sy_s, sy_r, sz_s, sz_r, sf_s, sf_r,
    rx_s, rx_r, ry_s, ry_r, r2_s, r2_r, r3_s, r3_r, core_s, core_r,
):
    own_rows, channels = lat_ref.shape
    width = own_rows * NZ
    groups = NX * NY
    blocks = groups // 2
    span = codes.shape[0]
    half = span // 2
    high = NZ // 2
    dp, code = lax.axis_index("dp"), lax.axis_index("code")
    x, y = lax.div(code, NY * high), lax.rem(lax.div(code, high), NY)
    low, core = lax.div(dp, 2), lax.rem(dp, 2)
    z = lax.rem(code, high) * 2 + low

    def at_x(k):
        return lax.rem(x + k, NX)

    def at_y(k):
        return lax.rem(y + k, NY)

    def at_z(k):
        return lax.rem(z + k, NZ)

    def device(px, py, pz, pc):
        return (lax.rem(pz, 2) * 2 + pc, (px * NY + py) * high + lax.div(pz, 2))

    def to_x(k):
        return device(at_x(k), y, z, core)

    def to_y(k):
        return device(x, at_y(k), z, core)

    def to_z(k):
        return device(x, y, at_z(k), core)

    twin = device(x, y, z, 1 - core)
    sent = []

    def push(src, dst, send, recv, target):
        copy = pltpu.make_async_remote_copy(
            src_ref=src, dst_ref=dst, send_sem=send, recv_sem=recv,
            device_id=target, device_id_type=MESH,
        )
        copy.start()
        sent.append(copy)
        return copy

    def arrive(copies):
        for copy in copies:
            copy.wait_recv()

    load = pltpu.make_async_copy(
        book_ref.at[pl.ds(pl.multiple_of(low * span, span), span)], wide, load_sem
    )
    load.start()
    quarter = pl.ds(pl.multiple_of(dp * half, half), half)
    adam_in = [
        pltpu.make_async_copy(src, adam.at[n], adam_s.at[n])
        for n, src in enumerate((book_ref.at[quarter], one_ref.at[0], two_ref.at[0]))
    ]
    for copy in adam_in:
        copy.start()

    barrier = pltpu.get_barrier_semaphore()
    partners = (
        [to_z(k) for k in range(1, NZ)]
        + [to_x(k) for k in range(1, NX)]
        + [to_y(k) for k in range(1, NY)]
        + [twin]
    )
    for partner in partners:
        pl.semaphore_signal(barrier, inc=1, device_id=partner, device_id_type=MESH)

    rows[0, x, y, z] = lat_ref[...]
    rows[1, x, y, z] = up_ref[...]
    lane = lax.broadcasted_iota(jnp.int32, (1, width), 1) - z * own_rows
    own_targets = jnp.zeros((1, width), jnp.int32)
    for k in range(own_rows):
        own_targets = jnp.where(lane == k, tgt_ref[k], own_targets)
    tgt_z[z] = own_targets
    pl.semaphore_wait(barrier, len(partners))

    far_first = sorted(range(1, NZ), key=lambda k: -min(k, NZ - k))
    first = [
        push(rows.at[:, x, y, z], rows.at[:, x, y, z], gz_s.at[k], gz_r.at[k], to_z(k))
        for k in far_first
    ] + [
        push(tgt_z.at[z], tgt_z.at[z], tz_s.at[k], tz_r.at[k], to_z(k)) for k in far_first
    ]
    load.wait()
    codes[...] = wide[...].astype(BF)
    codes_t[...] = wide[...].T.astype(BF)
    arrive(first)
    tgt_all[x, y] = jnp.sum(tgt_z[...], axis=0)
    tgt_two = [push(tgt_all.at[x, y], tgt_all.at[x, y], t2_s.at[k], t2_r.at[k], to_y(k)) for k in range(1, NY)]
    near_x = [1, NX - 1, 2] if NX > 2 else [1]
    near_y = [1, NY - 1, 2] if NY > 2 else [1]

    def lat_to_x(j, k):
        part = rows.at[0, x, at_y(j)]
        return push(part, part, gx_s.at[0, j, k], gx_r.at[0, j, k], to_x(k))

    def up_to_y(j, k):
        part = rows.at[1, at_x(j), y]
        return push(part, part, gx_s.at[1, j, k], gx_r.at[1, j, k], to_y(k))

    lat_two, up_two, lat_three, up_three = {}, {}, {}, {}
    for k in near_y:
        lat_two[k] = push(rows.at[0, x, y], rows.at[0, x, y], g2_s.at[0, k], g2_r.at[0, k], to_y(k))
    for k in near_x:
        up_two[k] = push(rows.at[1, x, y], rows.at[1, x, y], g2_s.at[1, k], g2_r.at[1, k], to_x(k))
    for k in near_x:
        lat_three[0, k] = lat_to_x(0, k)
    for k in near_y:
        up_three[0, k] = up_to_y(0, k)
    arrive(tgt_two)
    tgt_three = [push(tgt_all.at[x], tgt_all.at[x], t3_s.at[k], t3_r.at[k], to_x(k)) for k in range(1, NX)]
    for n in range(max(len(near_x), len(near_y))):
        if n < len(near_y):
            arrive([lat_two[near_y[n]]])
            for k in near_x:
                lat_three[NY - near_y[n], k] = lat_to_x(NY - near_y[n], k)
        if n < len(near_x):
            arrive([up_two[near_x[n]]])
            for k in near_y:
                up_three[NX - near_x[n], k] = up_to_y(NX - near_x[n], k)

    pairs = NY // 2

    def row_block(part, px, py):
        return rows[part, px, pl.ds(py, 2)].reshape(2 * width, channels)

    def piece(c):
        return pl.ds(c * chunk, chunk)

    pieces = span // chunk

    def pair_rows(part, pair):
        return jnp.concatenate(
            [rows[part, px, py].reshape(width, channels) for px, py in pair], axis=0
        )

    def scores(pair):
        (g, px, py), (h, qx, qy) = [(cx * NY + cy, cx, cy) for cx, cy in pair]
        lat_b = pair_rows(0, pair)
        peak = jnp.full((16, 2 * width), -jnp.inf, F32)
        for c in range(pieces):
            s = rows_dot(codes[piece(c)], lat_b)
            expo[g, piece(c)] = s[:, :width]
            expo[h, piece(c)] = s[:, width:]
            peak = jnp.maximum(peak, fold_rows(s, jnp.max))
        peak = jnp.max(peak, axis=0, keepdims=True)
        stat_own[px, 0, py] = peak[:, :width]
        stat_own[qx, 0, qy] = peak[:, width:]
        return peak

    def sums(pair, peak):
        (g, px, py), (h, qx, qy) = [(cx * NY + cy, cx, cy) for cx, cy in pair]
        up_b = pair_rows(1, pair)
        shift = peak * SCALE
        mass = jnp.zeros((16, 2 * width), F32)
        weighted = jnp.zeros((16, 2 * width), F32)
        for c in range(pieces):
            a = rows_dot(codes[piece(c)], up_b)
            s = jnp.concatenate([expo[g, piece(c)], expo[h, piece(c)]], axis=1)
            e = jnp.exp2(s * SCALE - shift)
            expo[g, piece(c)] = e[:, :width]
            expo[h, piece(c)] = e[:, width:]
            aff[g, piece(c)] = a[:, :width]
            aff[h, piece(c)] = a[:, width:]
            mass = mass + fold_rows(e, jnp.sum)
            weighted = weighted + fold_rows(e * a, jnp.sum)
        mass = jnp.sum(mass, axis=0, keepdims=True)
        weighted = jnp.sum(weighted, axis=0, keepdims=True)
        for k, value in enumerate((mass, weighted)):
            stat_own[px, k + 1, py] = value[:, :width]
            stat_own[qx, k + 1, qy] = value[:, width:]

    def back_rows(out, px, py):
        g = px * NY + py
        pair = jnp.concatenate([weights[g], weights[g + 1]], axis=1)
        t = plain_dot(codes_t[...], pair).astype(BF)
        out[px, py] = t[:, :width]
        out[px, py + 1] = t[:, width:]

    def back_codes(part, at):
        where = pl.ds(pl.multiple_of(at, chunk), chunk)
        total = None
        for b in range(blocks):
            pair = jnp.concatenate([weights[2 * b, where], weights[2 * b + 1, where]], axis=1)
            term = plain_dot(pair, row_block(part, b // pairs, b % pairs * 2))
            total = term if total is None else total + term
        return total

    base = code * (2 * span) + low * span
    index = lax.broadcasted_iota(jnp.int32, (chunk, width), 0)

    def one_hot(b, carry):
        px, py = lax.div(b, pairs), lax.rem(b, pairs) * 2
        for side in range(2):
            local = tgt_all[px, py + side] - base
            for c in range(pieces):
                weights[2 * b + side, piece(c)] = jnp.where(index == local - c * chunk, 1.0, 0.0).astype(BF)
        back_rows(quant_out, px, py)
        return carry

    far_plane = (2, 1, 3, 0) if NX > 2 else (1, 0)
    side_c = channels // 2
    lower, upper = pl.ds(0, side_c), pl.ds(side_c, side_c)

    def send_plane(n, out, k):
        px = at_x(k)
        copies = []
        if k:
            copies.append(push(out.at[px, :, lower], rs_one.at[n, 0, x], rx_s.at[n, k], rx_r.at[n, k], to_x(k)))
        for j in range(1, NY):
            copies.append(
                push(out.at[px, at_y(j), upper], rs_one.at[n, 1, y, px], ry_s.at[n, k, j], ry_r.at[n, k, j], to_y(j))
            )
        return copies

    def reduce_one(n, out):
        for j in range(NY):
            total = out[x, j, lower].astype(F32)
            for k in range(1, NX):
                total = total + rs_one[n, 0, at_x(k), j].astype(F32)
            rs_mid[n, 0, j] = total.astype(BF)
        copies = [
            push(rs_mid.at[n, 0, at_y(k)], rs_two.at[n, 0, y], r2_s.at[n, 0, k], r2_r.at[n, 0, k], to_y(k))
            for k in range(1, NY)
        ]
        for j in range(NX):
            total = out[j, y, upper].astype(F32)
            for k in range(1, NY):
                total = total + rs_one[n, 1, at_y(k), j].astype(F32)
            rs_mid[n, 1, j] = total.astype(BF)
        return copies + [
            push(rs_mid.at[n, 1, at_x(k)], rs_two.at[n, 1, x], r2_s.at[n, 1, k], r2_r.at[n, 1, k], to_x(k))
            for k in range(1, NX)
        ]

    def reduce_two(n):
        left = rs_mid[n, 0, y].astype(F32)
        for k in range(1, NY):
            left = left + rs_two[n, 0, at_y(k)].astype(F32)
        right = rs_mid[n, 1, x].astype(F32)
        for k in range(1, NX):
            right = right + rs_two[n, 1, at_x(k)].astype(F32)
        total = jnp.concatenate([left, right], axis=0).T.astype(BF)
        rs_last[n] = total.reshape(NZ, own_rows, channels)
        return [
            push(rs_last.at[n, at_z(k)], rs_three.at[n, z], r3_s.at[n, k], r3_r.at[n, k], to_z(k))
            for k in far_first
        ]

    def reduce_three(n):
        total = rs_last[n, z].astype(F32)
        for k in range(1, NZ):
            total = total + rs_three[n, at_z(k)].astype(F32)
        return total

    def late(cell):
        rank = [k if k < 2 else NX - k + (NX if k == 2 else 0) for k in cell]
        return (min(cell) > 0) * max(rank), sum(rank)

    cells = sorted([(i, j) for i in range(NX) for j in range(NY)], key=late)
    here = set()

    def arrive_once(copy):
        if id(copy) not in here:
            here.add(id(copy))
            arrive([copy])

    for n in range(0, groups, 2):
        pair = [(at_x(i), at_y(j)) for i, j in cells[n : n + 2]]
        for i, j in cells[n : n + 2]:
            if i:
                arrive_once(lat_three[j, NX - i])
        peak = scores(pair)
        for i, j in cells[n : n + 2]:
            if j:
                arrive_once(up_three[i, NY - j])
        sums(pair, peak)
    arrive(tgt_three)

    sx = [push(stat_own.at[at_x(k)], stat_x.at[x], sx_s.at[k], sx_r.at[k], to_x(k)) for k in range(1, NX)]

    def picked(c, carry):
        at = c * chunk
        wide[pl.ds(pl.multiple_of(at, chunk), chunk)] = back_codes(1, at)
        return carry

    early = blocks * 5 // 8
    lax.fori_loop(0, early, one_hot, 0)
    arrive(sx)
    merged = merge_stats([stat_own[x]] + [stat_x[at_x(k)] for k in range(1, NX)])
    for k in range(3):
        stat_mid[0, k] = merged[k]
    sy = [push(stat_mid.at[0], stat_y.at[y], sy_s.at[k], sy_r.at[k], to_y(k)) for k in range(1, NY)]
    lax.fori_loop(early, blocks, one_hot, 0)
    arrive(sy)
    merged = merge_stats([merged] + [stat_y[at_y(k)] for k in range(1, NY)])
    for k in range(3):
        stat_mid[1, k] = merged[k]
    sz = [push(stat_mid.at[1], stat_z.at[z], sz_s.at[k], sz_r.at[k], to_z(k)) for k in far_first]
    quant_one = []
    for k in far_plane:
        quant_one += send_plane(1, quant_out, k)
    lax.fori_loop(0, pieces, picked, 0)
    arrive(sz)
    peak, mass, weighted = merge_stats([merged] + [stat_z[at_z(k)] for k in range(1, NZ)])
    for k, value in enumerate((peak, logit_scale / mass, weighted / mass)):
        stat_fin[x, k] = value
    sf = [push(stat_fin.at[x], stat_fin.at[x], sf_s.at[k], sf_r.at[k], to_x(k)) for k in range(1, NX)]

    def weigh(px):
        def body(j, carry):
            py = j * 2
            g = px * NY + py
            for side in range(2):
                fade = (
                    jnp.exp2((stat_own[px, 0, py + side] - stat_fin[px, 0, py + side]) * SCALE)
                    * stat_fin[px, 1, py + side]
                )
                mean = stat_fin[px, 2, py + side]
                for c in range(pieces):
                    w = expo[g + side, piece(c)] * fade * (aff[g + side, piece(c)] - mean)
                    weights[g + side, piece(c)] = w.astype(BF)
            back_rows(soft_out, px, py)
            return carry

        lax.fori_loop(0, pairs, body, 0)

    weigh(x)
    arrive(sf)
    soft_one = send_plane(0, soft_out, 0)
    for k in far_plane[:-1]:
        weigh(at_x(k))
        soft_one += send_plane(0, soft_out, k)
    arrive(quant_one)
    quant_two = reduce_one(1, quant_out)

    def grad_other(c, carry):
        at = (1 - core) * half + c * chunk
        where = pl.ds(pl.multiple_of(at, chunk), chunk)
        code_out[pl.ds(pl.multiple_of(c * chunk, chunk), chunk)] = (back_codes(0, at) + wide[where]).astype(BF)
        return carry

    lax.fori_loop(0, half // chunk, grad_other, 0)
    swap = push(code_out, code_in, core_s, core_r, twin)
    arrive(soft_one)
    soft_two = reduce_one(0, soft_out)

    def grad_own(c, carry):
        at = core * half + c * chunk
        where = pl.ds(pl.multiple_of(at, chunk), chunk)
        own_grad[pl.ds(pl.multiple_of(c * chunk, chunk), chunk)] = back_codes(0, at) + wide[where]
        return carry

    lax.fori_loop(0, half // chunk, grad_own, 0)
    arrive(quant_two)
    quant_three = reduce_two(1)
    arrive(soft_two)
    soft_three = reduce_two(0)
    for copy in adam_in:
        copy.wait()
    swap.wait_recv()

    def update(c, carry):
        where = pl.ds(pl.multiple_of(c * chunk, chunk), chunk)
        slope = own_grad[where] + code_in[where].astype(F32)
        fresh_one = beta_one * adam[1, where] + (1.0 - beta_one) * slope
        fresh_two = beta_two * adam[2, where] + (1.0 - beta_two) * slope * slope
        adam[1, where] = fresh_one
        adam[2, where] = fresh_two
        adam[0, where] = adam[0, where] - learn_rate * (fresh_one / (1.0 - beta_one**ADAM_STEP)) / (
            jnp.sqrt(fresh_two / (1.0 - beta_two**ADAM_STEP)) + adam_eps
        )
        return carry

    lax.fori_loop(0, half // chunk, update, 0)
    arrive(quant_three)
    terms_ref[1] = reduce_three(1)
    arrive(soft_three)
    terms_ref[0] = reduce_three(0)
    for copy in sent:
        copy.wait_send()


def exchange(latents, upstream, targets, codebook, moment_one, moment_two):
    own_rows, channels = latents.shape
    width = own_rows * NZ
    span = codebook.shape[0] // 2
    half = span // 2
    groups = NX * NY
    chunk = min(256, half)
    dma = pltpu.SemaphoreType.DMA
    side_c = channels // 2
    in_vmem = pl.BlockSpec(memory_space=pltpu.VMEM)
    anywhere = pl.BlockSpec(memory_space=pl.ANY)
    scratch = [
        pltpu.VMEM((2, NX, NY, NZ, own_rows, channels), BF),
        pltpu.VMEM((NZ, 1, width), jnp.int32),
        pltpu.VMEM((NX, NY, 1, width), jnp.int32),
        pltpu.VMEM((span, channels), F32),
        pltpu.VMEM((span, channels), BF),
        pltpu.VMEM((channels, span), BF),
        pltpu.VMEM((groups, span, width), F32),
        pltpu.VMEM((groups, span, width), F32),
        pltpu.VMEM((groups, span, width), BF),
        pltpu.VMEM((NX, NY, channels, width), BF),
        pltpu.VMEM((NX, NY, channels, width), BF),
        pltpu.VMEM((2, 2, NX, NY, side_c, width), BF),
        pltpu.VMEM((2, 2, NX, side_c, width), BF),
        pltpu.VMEM((2, 2, NX, side_c, width), BF),
        pltpu.VMEM((2, NZ, own_rows, channels), BF),
        pltpu.VMEM((2, NZ, own_rows, channels), BF),
        pltpu.VMEM((NX, 3, NY, 1, width), F32),
        pltpu.VMEM((NX, 3, NY, 1, width), F32),
        pltpu.VMEM((NY, 3, NY, 1, width), F32),
        pltpu.VMEM((NZ, 3, NY, 1, width), F32),
        pltpu.VMEM((2, 3, NY, 1, width), F32),
        pltpu.VMEM((NX, 3, NY, 1, width), F32),
        pltpu.VMEM((half, channels), BF),
        pltpu.VMEM((half, channels), BF),
        pltpu.VMEM((half, channels), F32),
        dma, dma((3,)),
        dma((NZ,)), dma((NZ,)), dma((2, NX)), dma((2, NX)), dma((2, NX, NX)), dma((2, NX, NX)),
        dma((NZ,)), dma((NZ,)), dma((NY,)), dma((NY,)), dma((NX,)), dma((NX,)),
        dma((NX,)), dma((NX,)), dma((NY,)), dma((NY,)), dma((NZ,)), dma((NZ,)), dma((NX,)), dma((NX,)),
        dma((2, NX)), dma((2, NX)), dma((2, NX, NY)), dma((2, NX, NY)),
        dma((2, 2, NX)), dma((2, 2, NX)), dma((2, NZ)), dma((2, NZ)),
        dma, dma,
    ]
    return pl.pallas_call(
        functools.partial(kernel, chunk),
        out_shape=(
            pltpu.VMEM((2, own_rows, channels), F32),
            pltpu.VMEM((3, half, channels), F32),
        ),
        in_specs=[in_vmem, in_vmem, pl.BlockSpec(memory_space=pltpu.SMEM), anywhere, anywhere, anywhere],
        out_specs=(in_vmem, in_vmem),
        scratch_shapes=scratch,
        compiler_params=pltpu.CompilerParams(
            collective_id=0, has_side_effects=True, vmem_limit_bytes=57 * 1024 * 1024
        ),
    )(latents, upstream, targets, codebook, moment_one, moment_two)


def finish(terms, lat, fresh, quant_ref, lat_ref, book_ref, one_ref, two_ref, sems):
    copies = [
        pltpu.make_async_copy(fresh.at[n], target.at[0], sems.at[n])
        for n, target in enumerate((book_ref, one_ref, two_ref))
    ]
    for copy in copies:
        copy.start()
    quant = terms[1]
    quant_ref[...] = quant.astype(BF)
    lat_ref[...] = terms[0] + commit_weight * (lat[...].astype(F32) - quant)
    for copy in copies:
        copy.wait()


def per_device(latents, upstream, targets, codebook, moment_one, moment_two):
    terms, fresh = exchange(latents, upstream, targets, codebook, moment_one, moment_two)
    in_vmem = pl.BlockSpec(memory_space=pltpu.VMEM)
    anywhere = pl.BlockSpec(memory_space=pl.ANY)
    moment = jax.ShapeDtypeStruct(moment_one.shape, F32)
    return pl.pallas_call(
        finish,
        out_shape=(
            jax.ShapeDtypeStruct(latents.shape, BF),
            jax.ShapeDtypeStruct(latents.shape, F32),
            moment, moment, moment,
        ),
        in_specs=[in_vmem, in_vmem, in_vmem],
        out_specs=(in_vmem, in_vmem, anywhere, anywhere, anywhere),
        scratch_shapes=[pltpu.SemaphoreType.DMA((3,))],
        compiler_params=pltpu.CompilerParams(vmem_limit_bytes=8 * 1024 * 1024),
    )(terms, latents, fresh)


def solution(mesh):
    return jax.shard_map(
        per_device,
        mesh=mesh,
        in_specs=(
            P(("dp", "code"), None),
            P(("dp", "code"), None),
            P(("dp", "code")),
            P("code", None),
            P("code", "dp", None),
            P("code", "dp", None),
        ),
        out_specs=(
            P(("dp", "code"), None),
            P(("dp", "code"), None),
            P("code", "dp", None),
            P("code", "dp", None),
            P("code", "dp", None),
        ),
        check_vma=False,
    )
```

```python
import functools

import jax
import jax.numpy as jnp
from jax import lax
from jax.experimental import pallas as pl
from jax.experimental.pallas import tpu as pltpu
from jax.sharding import PartitionSpec as P

ADAM_2 = 100
logit_scale = 4.0
commit_weight = 0.5
learn_rate = 0.001
beta_one = 0.9
beta_two = 0.999
adam_eps = 1e-08

NX, NY, NZ = 4, 4, 8
MESH = pl.DeviceIdType.MESH
LOG2E = 1.4426950408889634
SCALE = logit_scale * LOG2E
BF = jnp.bfloat16
F32 = jnp.float32


def rows_dot(lhs, rhs):
    return lax.dot_general(lhs, rhs, (((1,), (1,)), ((), ())), preferred_element_type=F32)


def plain_dot(lhs, rhs):
    return jnp.dot(lhs, rhs, preferred_element_type=F32)


def fold_rows(block, op):
    return op(block.reshape(block.shape[0] // 16, 16, block.shape[1]), axis=0)


def merge_stats(parts):
    peak = functools.reduce(jnp.maximum, [part[0] for part in parts])
    fades = [jnp.exp2((part[0] - peak) * SCALE) for part in parts]
    mass = sum(part[1] * fade for part, fade in zip(parts, fades))
    weighted = sum(part[2] * fade for part, fade in zip(parts, fades))
    return peak, mass, weighted


def kernel(
    chunk,
    lat_ref, up_ref, tgt_ref, book_ref, one_ref, two_ref,
    terms_ref, adam,
    rows, tgt_z, tgt_all, wide, codes, codes_t, expo, aff, weights,
    soft_out, quant_out, rs_one, rs_two, rs_mid, rs_last, rs_three,
    stat_own, stat_x, stat_y, stat_z, stat_mid, stat_fin, code_out, code_in, own_grad,
    load_sem, adam_s, gz_s, gz_r, g2_s, g2_r, gx_s, gx_r, tz_s, tz_r, t2_s, t2_r, t3_s, t3_r,
    sx_s, sx_r, sy_s, sy_r, sz_s, sz_r, sf_s, sf_r,
    rx_s, rx_r, ry_s, ry_r, r2_s, r2_r, r3_s, r3_r, core_s, core_r,
):
    own_rows, channels = lat_ref.shape
    width = own_rows * NZ
    groups = NX * NY
    blocks = groups // 2
    span = codes.shape[0]
    half = span // 2
    high = NZ // 2
    dp, code = lax.axis_index("dp"), lax.axis_index("code")
    x, y = lax.div(code, NY * high), lax.rem(lax.div(code, high), NY)
    low, core = lax.div(dp, 2), lax.rem(dp, 2)
    z = lax.rem(code, high) * 2 + low

    def at_x(k):
        return lax.rem(x + k, NX)

    def at_y(k):
        return lax.rem(y + k, NY)

    def at_z(k):
        return lax.rem(z + k, NZ)

    def device(px, py, pz, pc):
        return (lax.rem(pz, 2) * 2 + pc, (px * NY + py) * high + lax.div(pz, 2))

    def to_x(k):
        return device(at_x(k), y, z, core)

    def to_y(k):
        return device(x, at_y(k), z, core)

    def to_z(k):
        return device(x, y, at_z(k), core)

    twin = device(x, y, z, 1 - core)
    sent = []

    def push(src, dst, send, recv, target):
        copy = pltpu.make_async_remote_copy(
            src_ref=src, dst_ref=dst, send_sem=send, recv_sem=recv,
            device_id=target, device_id_type=MESH,
        )
        copy.start()
        sent.append(copy)
        return copy

    def arrive(copies):
        for copy in copies:
            copy.wait_recv()

    load = pltpu.make_async_copy(
        book_ref.at[pl.ds(pl.multiple_of(low * span, span), span)], wide, load_sem
    )
    load.start()
    quarter = pl.ds(pl.multiple_of(dp * half, half), half)
    adam_in = [
        pltpu.make_async_copy(src, adam.at[n], adam_s.at[n])
        for n, src in enumerate((book_ref.at[quarter], one_ref.at[0], two_ref.at[0]))
    ]
    for copy in adam_in:
        copy.start()

    barrier = pltpu.get_barrier_semaphore()
    partners = (
        [to_z(k) for k in range(1, NZ)]
        + [to_x(k) for k in range(1, NX)]
        + [to_y(k) for k in range(1, NY)]
        + [twin]
    )
    for partner in partners:
        pl.semaphore_signal(barrier, inc=1, device_id=partner, device_id_type=MESH)

    rows[0, x, y, z] = lat_ref[...]
    rows[1, x, y, z] = up_ref[...]
    lane = lax.broadcasted_iota(jnp.int32, (1, width), 1) - z * own_rows
    own_targets = jnp.zeros((1, width), jnp.int32)
    for k in range(own_rows):
        own_targets = jnp.where(lane == k, tgt_ref[k], own_targets)
    tgt_z[z] = own_targets
    pl.semaphore_wait(barrier, len(partners))

    far_first = sorted(range(1, NZ), key=lambda k: -min(k, NZ - k))
    first = [
        push(rows.at[:, x, y, z], rows.at[:, x, y, z], gz_s.at[k], gz_r.at[k], to_z(k))
        for k in far_first
    ] + [
        push(tgt_z.at[z], tgt_z.at[z], tz_s.at[k], tz_r.at[k], to_z(k)) for k in far_first
    ]
    load.wait()
    codes[...] = wide[...].astype(BF)
    codes_t[...] = wide[...].T.astype(BF)
    arrive(first)
    tgt_all[x, y] = jnp.sum(tgt_z[...], axis=0)
    tgt_two = [push(tgt_all.at[x, y], tgt_all.at[x, y], t2_s.at[k], t2_r.at[k], to_y(k)) for k in range(1, NY)]
    near_x = [1, NX - 1, 2] if NX > 2 else [1]
    near_y = [1, NY - 1, 2] if NY > 2 else [1]

    def lat_to_x(j, k):
        part = rows.at[0, x, at_y(j)]
        return push(part, part, gx_s.at[0, j, k], gx_r.at[0, j, k], to_x(k))

    def up_to_y(j, k):
        part = rows.at[1, at_x(j), y]
        return push(part, part, gx_s.at[1, j, k], gx_r.at[1, j, k], to_y(k))

    lat_two, up_two, lat_three, up_three = {}, {}, {}, {}
    for k in near_y:
        lat_two[k] = push(rows.at[0, x, y], rows.at[0, x, y], g2_s.at[0, k], g2_r.at[0, k], to_y(k))
    for k in near_x:
        up_two[k] = push(rows.at[1, x, y], rows.at[1, x, y], g2_s.at[1, k], g2_r.at[1, k], to_x(k))
    for k in near_x:
        lat_three[0, k] = lat_to_x(0, k)
    for k in near_y:
        up_three[0, k] = up_to_y(0, k)
    arrive(tgt_two)
    tgt_three = [push(tgt_all.at[x], tgt_all.at[x], t3_s.at[k], t3_r.at[k], to_x(k)) for k in range(1, NX)]
    for n in range(max(len(near_x), len(near_y))):
        if n < len(near_y):
            arrive([lat_two[near_y[n]]])
            for k in near_x:
                lat_three[NY - near_y[n], k] = lat_to_x(NY - near_y[n], k)
        if n < len(near_x):
            arrive([up_two[near_x[n]]])
            for k in near_y:
                up_three[NX - near_x[n], k] = up_to_y(NX - near_x[n], k)

    pairs = NY // 2

    def row_block(part, px, py):
        return rows[part, px, pl.ds(py, 2)].reshape(2 * width, channels)

    def piece(c):
        return pl.ds(c * chunk, chunk)

    pieces = span // chunk

    def pair_rows(part, pair):
        return jnp.concatenate(
            [rows[part, px, py].reshape(width, channels) for px, py in pair], axis=0
        )

    def group(cell):
        return cell[0] * NY + cell[1]

    def local_stats(pair, peak, ahead):
        if ahead:
            lat_n = pair_rows(0, ahead)
            peak_n = jnp.full((16, 2 * width), -jnp.inf, F32)
        if pair:
            g, h = group(pair[0]), group(pair[1])
            up_b = pair_rows(1, pair)
            lat_b = pair_rows(0, pair)
            shift = peak * SCALE
            mass = jnp.zeros((16, 2 * width), F32)
            weighted = jnp.zeros((16, 2 * width), F32)
        for c in range(pieces):
            if ahead:
                s = rows_dot(codes[piece(c)], lat_n)
                peak_n = jnp.maximum(peak_n, fold_rows(s, jnp.max))
            if pair:
                a = rows_dot(codes[piece(c)], up_b)
                s = rows_dot(codes[piece(c)], lat_b)
                e = jnp.exp2(s * SCALE - shift)
                expo[g, piece(c)] = e[:, :width]
                expo[h, piece(c)] = e[:, width:]
                aff[g, piece(c)] = a[:, :width]
                aff[h, piece(c)] = a[:, width:]
                mass = mass + fold_rows(e, jnp.sum)
                weighted = weighted + fold_rows(e * a, jnp.sum)
        if pair:
            mass = jnp.sum(mass, axis=0, keepdims=True)
            weighted = jnp.sum(weighted, axis=0, keepdims=True)
            for k, value in enumerate((peak, mass, weighted)):
                for n, (px, py) in enumerate(pair):
                    stat_own[px, k, py] = value[:, n * width : (n + 1) * width]
        return jnp.max(peak_n, axis=0, keepdims=True) if ahead else None

    def back_rows(out, px, py):
        g = px * NY + py
        pair = jnp.concatenate([weights[g], weights[g + 1]], axis=1)
        t = plain_dot(codes_t[...], pair).astype(BF)
        out[px, py] = t[:, :width]
        out[px, py + 1] = t[:, width:]

    def back_codes(part, at):
        where = pl.ds(pl.multiple_of(at, chunk), chunk)
        total = None
        for b in range(blocks):
            pair = jnp.concatenate([weights[2 * b, where], weights[2 * b + 1, where]], axis=1)
            term = plain_dot(pair, row_block(part, b // pairs, b % pairs * 2))
            total = term if total is None else total + term
        return total

    base = code * (2 * span) + low * span
    index = lax.broadcasted_iota(jnp.int32, (chunk, width), 0)

    def one_hot(b, carry):
        px, py = lax.div(b, pairs), lax.rem(b, pairs) * 2
        for side in range(2):
            local = tgt_all[px, py + side] - base
            for c in range(pieces):
                weights[2 * b + side, piece(c)] = jnp.where(index == local - c * chunk, 1.0, 0.0).astype(BF)
        back_rows(quant_out, px, py)
        return carry

    far_plane = (2, 1, 3, 0) if NX > 2 else (1, 0)
    side_c = channels // 2
    lower, upper = pl.ds(0, side_c), pl.ds(side_c, side_c)

    def send_plane(n, out, k):
        px = at_x(k)
        copies = []
        if k:
            copies.append(push(out.at[px, :, lower], rs_one.at[n, 0, x], rx_s.at[n, k], rx_r.at[n, k], to_x(k)))
        for j in range(1, NY):
            copies.append(
                push(out.at[px, at_y(j), upper], rs_one.at[n, 1, y, px], ry_s.at[n, k, j], ry_r.at[n, k, j], to_y(j))
            )
        return copies

    def reduce_one(n, out):
        for j in range(NY):
            total = out[x, j, lower].astype(F32)
            for k in range(1, NX):
                total = total + rs_one[n, 0, at_x(k), j].astype(F32)
            rs_mid[n, 0, j] = total.astype(BF)
        copies = [
            push(rs_mid.at[n, 0, at_y(k)], rs_two.at[n, 0, y], r2_s.at[n, 0, k], r2_r.at[n, 0, k], to_y(k))
            for k in range(1, NY)
        ]
        for j in range(NX):
            total = out[j, y, upper].astype(F32)
            for k in range(1, NY):
                total = total + rs_one[n, 1, at_y(k), j].astype(F32)
            rs_mid[n, 1, j] = total.astype(BF)
        return copies + [
            push(rs_mid.at[n, 1, at_x(k)], rs_two.at[n, 1, x], r2_s.at[n, 1, k], r2_r.at[n, 1, k], to_x(k))
            for k in range(1, NX)
        ]

    def reduce_two(n):
        left = rs_mid[n, 0, y].astype(F32)
        for k in range(1, NY):
            left = left + rs_two[n, 0, at_y(k)].astype(F32)
        right = rs_mid[n, 1, x].astype(F32)
        for k in range(1, NX):
            right = right + rs_two[n, 1, at_x(k)].astype(F32)
        total = jnp.concatenate([left, right], axis=0).T.astype(BF)
        rs_last[n] = total.reshape(NZ, own_rows, channels)
        return [
            push(rs_last.at[n, at_z(k)], rs_three.at[n, z], r3_s.at[n, k], r3_r.at[n, k], to_z(k))
            for k in far_first
        ]

    def reduce_three(n):
        total = rs_last[n, z].astype(F32)
        for k in range(1, NZ):
            total = total + rs_three[n, at_z(k)].astype(F32)
        return total

    def late(cell):
        rank = [k if k < 2 else NX - k + (NX if k == 2 else 0) for k in cell]
        return (min(cell) > 0) * max(rank), sum(rank)

    cells = sorted([(i, j) for i in range(NX) for j in range(NY)], key=late)
    here = set()

    def arrive_once(copy):
        if id(copy) not in here:
            here.add(id(copy))
            arrive([copy])

    pair, peak = None, None
    for n in range(0, groups + 2, 2):
        for i, j in cells[n : n + 2]:
            if i:
                arrive_once(lat_three[j, NX - i])
        for i, j in cells[n - 2 : n] if n else ():
            if j:
                arrive_once(up_three[i, NY - j])
        ahead = [(at_x(i), at_y(j)) for i, j in cells[n : n + 2]]
        peak = local_stats(pair, peak, ahead)
        pair = ahead
    arrive(tgt_three)

    sx = [push(stat_own.at[at_x(k)], stat_x.at[x], sx_s.at[k], sx_r.at[k], to_x(k)) for k in range(1, NX)]

    def picked(c, carry):
        at = c * chunk
        wide[pl.ds(pl.multiple_of(at, chunk), chunk)] = back_codes(1, at)
        return carry

    early = blocks * 5 // 8
    lax.fori_loop(0, early, one_hot, 0)
    arrive(sx)
    merged = merge_stats([stat_own[x]] + [stat_x[at_x(k)] for k in range(1, NX)])
    for k in range(3):
        stat_mid[0, k] = merged[k]
    sy = [push(stat_mid.at[0], stat_y.at[y], sy_s.at[k], sy_r.at[k], to_y(k)) for k in range(1, NY)]
    lax.fori_loop(early, blocks, one_hot, 0)
    arrive(sy)
    merged = merge_stats([merged] + [stat_y[at_y(k)] for k in range(1, NY)])
    for k in range(3):
        stat_mid[1, k] = merged[k]
    sz = [push(stat_mid.at[1], stat_z.at[z], sz_s.at[k], sz_r.at[k], to_z(k)) for k in far_first]
    quant_one = []
    for k in far_plane:
        quant_one += send_plane(1, quant_out, k)
    lax.fori_loop(0, pieces, picked, 0)
    arrive(sz)
    peak, mass, weighted = merge_stats([merged] + [stat_z[at_z(k)] for k in range(1, NZ)])
    for k, value in enumerate((peak, logit_scale / mass, weighted / mass)):
        stat_fin[x, k] = value
    sf = [push(stat_fin.at[x], stat_fin.at[x], sf_s.at[k], sf_r.at[k], to_x(k)) for k in range(1, NX)]

    def weigh(px):
        def body(j, carry):
            py = j * 2
            g = px * NY + py
            fade, mean = [], []
            for side in range(2):
                fade.append(
                    jnp.exp2((stat_own[px, 0, py + side] - stat_fin[px, 0, py + side]) * SCALE)
                    * stat_fin[px, 1, py + side]
                )
                mean.append(stat_fin[px, 2, py + side])
            total = None
            for c in range(0, pieces, 2):
                pair = []
                for side in range(2):
                    parts = []
                    for d in range(c, c + 2):
                        w = expo[g + side, piece(d)] * fade[side] * (aff[g + side, piece(d)] - mean[side])
                        weights[g + side, piece(d)] = w.astype(BF)
                        parts.append(w.astype(BF))
                    pair.append(jnp.concatenate(parts, axis=0))
                term = plain_dot(codes_t[:, c * chunk : (c + 2) * chunk], jnp.concatenate(pair, axis=1))
                total = term if total is None else total + term
            total = total.astype(BF)
            soft_out[px, py] = total[:, :width]
            soft_out[px, py + 1] = total[:, width:]
            return carry

        lax.fori_loop(0, pairs, body, 0)

    weigh(x)
    arrive(sf)
    soft_one = send_plane(0, soft_out, 0)
    for k in far_plane[:-1]:
        weigh(at_x(k))
        soft_one += send_plane(0, soft_out, k)
    arrive(quant_one)
    quant_two = reduce_one(1, quant_out)

    def grad_other(c, carry):
        at = (1 - core) * half + c * chunk
        where = pl.ds(pl.multiple_of(at, chunk), chunk)
        code_out[pl.ds(pl.multiple_of(c * chunk, chunk), chunk)] = (back_codes(0, at) + wide[where]).astype(BF)
        return carry

    lax.fori_loop(0, half // chunk, grad_other, 0)
    swap = push(code_out, code_in, core_s, core_r, twin)
    arrive(soft_one)
    soft_two = reduce_one(0, soft_out)

    def grad_own(c, carry):
        at = core * half + c * chunk
        where = pl.ds(pl.multiple_of(at, chunk), chunk)
        own_grad[pl.ds(pl.multiple_of(c * chunk, chunk), chunk)] = back_codes(0, at) + wide[where]
        return carry

    lax.fori_loop(0, half // chunk, grad_own, 0)
    arrive(quant_two)
    quant_three = reduce_two(1)
    arrive(soft_two)
    soft_three = reduce_two(0)
    for copy in adam_in:
        copy.wait()
    swap.wait_recv()

    def update(c, carry):
        where = pl.ds(pl.multiple_of(c * chunk, chunk), chunk)
        slope = own_grad[where] + code_in[where].astype(F32)
        fresh_one = beta_one * adam[1, where] + (1.0 - beta_one) * slope
        fresh_two = beta_two * adam[2, where] + (1.0 - beta_two) * slope * slope
        adam[1, where] = fresh_one
        adam[2, where] = fresh_two
        adam[0, where] = adam[0, where] - learn_rate * (fresh_one / (1.0 - beta_one**ADAM_2)) / (
            jnp.sqrt(fresh_two / (1.0 - beta_two**ADAM_2)) + adam_eps
        )
        return carry

    lax.fori_loop(0, half // chunk, update, 0)
    arrive(quant_three)
    terms_ref[1] = reduce_three(1)
    arrive(soft_three)
    terms_ref[0] = reduce_three(0)
    for copy in sent:
        copy.wait_send()


def exchange(latents, upstream, targets, codebook, moment_one, moment_two):
    own_rows, channels = latents.shape
    width = own_rows * NZ
    span = codebook.shape[0] // 2
    half = span // 2
    groups = NX * NY
    chunk = min(256, half)
    dma = pltpu.SemaphoreType.DMA
    side_c = channels // 2
    in_vmem = pl.BlockSpec(memory_space=pltpu.VMEM)
    anywhere = pl.BlockSpec(memory_space=pl.ANY)
    scratch = [
        pltpu.VMEM((2, NX, NY, NZ, own_rows, channels), BF),
        pltpu.VMEM((NZ, 1, width), jnp.int32),
        pltpu.VMEM((NX, NY, 1, width), jnp.int32),
        pltpu.VMEM((span, channels), F32),
        pltpu.VMEM((span, channels), BF),
        pltpu.VMEM((channels, span), BF),
        pltpu.VMEM((groups, span, width), F32),
        pltpu.VMEM((groups, span, width), F32),
        pltpu.VMEM((groups, span, width), BF),
        pltpu.VMEM((NX, NY, channels, width), BF),
        pltpu.VMEM((NX, NY, channels, width), BF),
        pltpu.VMEM((2, 2, NX, NY, side_c, width), BF),
        pltpu.VMEM((2, 2, NX, side_c, width), BF),
        pltpu.VMEM((2, 2, NX, side_c, width), BF),
        pltpu.VMEM((2, NZ, own_rows, channels), BF),
        pltpu.VMEM((2, NZ, own_rows, channels), BF),
        pltpu.VMEM((NX, 3, NY, 1, width), F32),
        pltpu.VMEM((NX, 3, NY, 1, width), F32),
        pltpu.VMEM((NY, 3, NY, 1, width), F32),
        pltpu.VMEM((NZ, 3, NY, 1, width), F32),
        pltpu.VMEM((2, 3, NY, 1, width), F32),
        pltpu.VMEM((NX, 3, NY, 1, width), F32),
        pltpu.VMEM((half, channels), BF),
        pltpu.VMEM((half, channels), BF),
        pltpu.VMEM((half, channels), F32),
        dma, dma((3,)),
        dma((NZ,)), dma((NZ,)), dma((2, NX)), dma((2, NX)), dma((2, NX, NX)), dma((2, NX, NX)),
        dma((NZ,)), dma((NZ,)), dma((NY,)), dma((NY,)), dma((NX,)), dma((NX,)),
        dma((NX,)), dma((NX,)), dma((NY,)), dma((NY,)), dma((NZ,)), dma((NZ,)), dma((NX,)), dma((NX,)),
        dma((2, NX)), dma((2, NX)), dma((2, NX, NY)), dma((2, NX, NY)),
        dma((2, 2, NX)), dma((2, 2, NX)), dma((2, NZ)), dma((2, NZ)),
        dma, dma,
    ]
    return pl.pallas_call(
        functools.partial(kernel, chunk),
        out_shape=(
            pltpu.VMEM((2, own_rows, channels), F32),
            pltpu.VMEM((3, half, channels), F32),
        ),
        in_specs=[in_vmem, in_vmem, pl.BlockSpec(memory_space=pltpu.SMEM), anywhere, anywhere, anywhere],
        out_specs=(in_vmem, in_vmem),
        scratch_shapes=scratch,
        compiler_params=pltpu.CompilerParams(
            collective_id=0, has_side_effects=True, vmem_limit_bytes=57 * 1024 * 1024
        ),
    )(latents, upstream, targets, codebook, moment_one, moment_two)


def finish(terms, lat, fresh, quant_ref, lat_ref, book_ref, one_ref, two_ref, sems):
    copies = [
        pltpu.make_async_copy(fresh.at[n], target.at[0], sems.at[n])
        for n, target in enumerate((book_ref, one_ref, two_ref))
    ]
    for copy in copies:
        copy.start()
    quant = terms[1]
    quant_ref[...] = quant.astype(BF)
    lat_ref[...] = terms[0] + commit_weight * (lat[...].astype(F32) - quant)
    for copy in copies:
        copy.wait()


def per_device(latents, upstream, targets, codebook, moment_one, moment_two):
    terms, fresh = exchange(latents, upstream, targets, codebook, moment_one, moment_two)
    in_vmem = pl.BlockSpec(memory_space=pltpu.VMEM)
    anywhere = pl.BlockSpec(memory_space=pl.ANY)
    moment = jax.ShapeDtypeStruct(moment_one.shape, F32)
    return pl.pallas_call(
        finish,
        out_shape=(
            jax.ShapeDtypeStruct(latents.shape, BF),
            jax.ShapeDtypeStruct(latents.shape, F32),
            moment, moment, moment,
        ),
        in_specs=[in_vmem, in_vmem, in_vmem],
        out_specs=(in_vmem, in_vmem, anywhere, anywhere, anywhere),
        scratch_shapes=[pltpu.SemaphoreType.DMA((3,))],
        compiler_params=pltpu.CompilerParams(vmem_limit_bytes=8 * 1024 * 1024),
    )(terms, latents, fresh)


def solution(mesh):
    return jax.shard_map(
        per_device,
        mesh=mesh,
        in_specs=(
            P(("dp", "code"), None),
            P(("dp", "code"), None),
            P(("dp", "code")),
            P("code", None),
            P("code", "dp", None),
            P("code", "dp", None),
        ),
        out_specs=(
            P(("dp", "code"), None),
            P(("dp", "code"), None),
            P("code", "dp", None),
            P("code", "dp", None),
            P("code", "dp", None),
        ),
        check_vma=False,
    )
```

```python
import functools

import jax
import jax.numpy as jnp
from jax import lax
from jax.experimental import pallas as pl
from jax.experimental.pallas import tpu as pltpu
from jax.sharding import PartitionSpec as P

ADAM_2 = 100
logit_scale = 4.0
commit_weight = 0.5
learn_rate = 0.001
beta_one = 0.9
beta_two = 0.999
adam_eps = 1e-08

NX, NY, NZ = 4, 4, 8
MESH = pl.DeviceIdType.MESH
LOG2E = 1.4426950408889634
SCALE = logit_scale * LOG2E
BF = jnp.bfloat16
F32 = jnp.float32


def rows_dot(lhs, rhs):
    return lax.dot_general(lhs, rhs, (((1,), (1,)), ((), ())), preferred_element_type=F32)


def plain_dot(lhs, rhs):
    return jnp.dot(lhs, rhs, preferred_element_type=F32)


def fold_rows(block, op):
    return op(block.reshape(block.shape[0] // 16, 16, block.shape[1]), axis=0)


def merge_stats(parts):
    peak = functools.reduce(jnp.maximum, [part[0] for part in parts])
    fades = [jnp.exp2((part[0] - peak) * SCALE) for part in parts]
    mass = sum(part[1] * fade for part, fade in zip(parts, fades))
    weighted = sum(part[2] * fade for part, fade in zip(parts, fades))
    return peak, mass, weighted


def kernel(
    chunk,
    lat_ref, up_ref, tgt_ref, book_ref, one_ref, two_ref,
    terms_ref, adam,
    rows, tgt_z, tgt_all, wide, codes, codes_t, expo, aff, weights,
    soft_out, quant_out, rs_one, rs_two, rs_mid, rs_last, rs_three,
    stat_own, stat_x, stat_y, stat_z, stat_mid, stat_fin, code_out, code_in, own_grad,
    load_sem, adam_s, gz_s, gz_r, g2_s, g2_r, gx_s, gx_r, tz_s, tz_r, t2_s, t2_r, t3_s, t3_r,
    sx_s, sx_r, sy_s, sy_r, sz_s, sz_r, sf_s, sf_r,
    rx_s, rx_r, ry_s, ry_r, r2_s, r2_r, r3_s, r3_r, core_s, core_r,
):
    own_rows, channels = lat_ref.shape
    width = own_rows * NZ
    groups = NX * NY
    blocks = groups // 2
    span = codes.shape[0]
    half = span // 2
    high = NZ // 2
    dp, code = lax.axis_index("dp"), lax.axis_index("code")
    x, y = lax.div(code, NY * high), lax.rem(lax.div(code, high), NY)
    low, core = lax.div(dp, 2), lax.rem(dp, 2)
    z = lax.rem(code, high) * 2 + low

    def at_x(k):
        return lax.rem(x + k, NX)

    def at_y(k):
        return lax.rem(y + k, NY)

    def at_z(k):
        return lax.rem(z + k, NZ)

    def device(px, py, pz, pc):
        return (lax.rem(pz, 2) * 2 + pc, (px * NY + py) * high + lax.div(pz, 2))

    def to_x(k):
        return device(at_x(k), y, z, core)

    def to_y(k):
        return device(x, at_y(k), z, core)

    def to_z(k):
        return device(x, y, at_z(k), core)

    twin = device(x, y, z, 1 - core)
    sent = []

    def push(src, dst, send, recv, target):
        copy = pltpu.make_async_remote_copy(
            src_ref=src, dst_ref=dst, send_sem=send, recv_sem=recv,
            device_id=target, device_id_type=MESH,
        )
        copy.start()
        sent.append(copy)
        return copy

    def arrive(copies):
        for copy in copies:
            copy.wait_recv()

    load = pltpu.make_async_copy(
        book_ref.at[pl.ds(pl.multiple_of(low * span, span), span)], wide, load_sem
    )
    load.start()
    quarter = pl.ds(pl.multiple_of(dp * half, half), half)
    adam_in = [
        pltpu.make_async_copy(src, adam.at[n], adam_s.at[n])
        for n, src in enumerate((book_ref.at[quarter], one_ref.at[0], two_ref.at[0]))
    ]
    for copy in adam_in:
        copy.start()

    barrier = pltpu.get_barrier_semaphore()
    partners = (
        [to_z(k) for k in range(1, NZ)]
        + [to_x(k) for k in range(1, NX)]
        + [to_y(k) for k in range(1, NY)]
        + [twin]
    )
    for partner in partners:
        pl.semaphore_signal(barrier, inc=1, device_id=partner, device_id_type=MESH)

    rows[0, x, y, z] = lat_ref[...]
    rows[1, x, y, z] = up_ref[...]
    lane = lax.broadcasted_iota(jnp.int32, (1, width), 1) - z * own_rows
    own_targets = jnp.zeros((1, width), jnp.int32)
    for k in range(own_rows):
        own_targets = jnp.where(lane == k, tgt_ref[k], own_targets)
    tgt_z[z] = own_targets
    pl.semaphore_wait(barrier, len(partners))

    far_first = sorted(range(1, NZ), key=lambda k: -min(k, NZ - k))
    first = [
        push(rows.at[:, x, y, z], rows.at[:, x, y, z], gz_s.at[k], gz_r.at[k], to_z(k))
        for k in far_first
    ] + [
        push(tgt_z.at[z], tgt_z.at[z], tz_s.at[k], tz_r.at[k], to_z(k)) for k in far_first
    ]
    load.wait()
    codes[...] = wide[...].astype(BF)
    codes_t[...] = wide[...].T.astype(BF)
    arrive(first)
    tgt_all[x, y] = jnp.sum(tgt_z[...], axis=0)
    tgt_two = [push(tgt_all.at[x, y], tgt_all.at[x, y], t2_s.at[k], t2_r.at[k], to_y(k)) for k in range(1, NY)]
    near_x = [1, NX - 1, 2] if NX > 2 else [1]
    near_y = [1, NY - 1, 2] if NY > 2 else [1]

    def lat_to_x(j, k):
        part = rows.at[0, x, at_y(j)]
        return push(part, part, gx_s.at[0, j, k], gx_r.at[0, j, k], to_x(k))

    def up_to_y(j, k):
        part = rows.at[1, at_x(j), y]
        return push(part, part, gx_s.at[1, j, k], gx_r.at[1, j, k], to_y(k))

    lat_two, up_two, lat_three, up_three = {}, {}, {}, {}
    for k in near_y:
        lat_two[k] = push(rows.at[0, x, y], rows.at[0, x, y], g2_s.at[0, k], g2_r.at[0, k], to_y(k))
    for k in near_x:
        up_two[k] = push(rows.at[1, x, y], rows.at[1, x, y], g2_s.at[1, k], g2_r.at[1, k], to_x(k))
    for k in near_x:
        lat_three[0, k] = lat_to_x(0, k)
    for k in near_y:
        up_three[0, k] = up_to_y(0, k)
    arrive(tgt_two)
    tgt_three = [push(tgt_all.at[x], tgt_all.at[x], t3_s.at[k], t3_r.at[k], to_x(k)) for k in range(1, NX)]
    for n in range(max(len(near_x), len(near_y))):
        if n < len(near_y):
            arrive([lat_two[near_y[n]]])
            for k in near_x:
                lat_three[NY - near_y[n], k] = lat_to_x(NY - near_y[n], k)
        if n < len(near_x):
            arrive([up_two[near_x[n]]])
            for k in near_y:
                up_three[NX - near_x[n], k] = up_to_y(NX - near_x[n], k)

    pairs = NY // 2

    def row_block(part, px, py):
        return rows[part, px, pl.ds(py, 2)].reshape(2 * width, channels)

    def piece(c):
        return pl.ds(c * chunk, chunk)

    pieces = span // chunk

    def pair_rows(part, pair):
        return jnp.concatenate(
            [rows[part, px, py].reshape(width, channels) for px, py in pair], axis=0
        )

    def group(cell):
        return cell[0] * NY + cell[1]

    def local_stats(pair, peak, ahead):
        if ahead:
            lat_n = pair_rows(0, ahead)
            peak_n = jnp.full((16, 2 * width), -jnp.inf, F32)
        if pair:
            g, h = group(pair[0]), group(pair[1])
            up_b = pair_rows(1, pair)
            lat_b = pair_rows(0, pair)
            shift = peak * SCALE
            mass = jnp.zeros((16, 2 * width), F32)
            weighted = jnp.zeros((16, 2 * width), F32)
        for c in range(pieces):
            if ahead:
                s = rows_dot(codes[piece(c)], lat_n)
                peak_n = jnp.maximum(peak_n, fold_rows(s, jnp.max))
            if pair:
                a = rows_dot(codes[piece(c)], up_b)
                s = rows_dot(codes[piece(c)], lat_b)
                e = jnp.exp2(s * SCALE - shift)
                expo[g, piece(c)] = e[:, :width]
                expo[h, piece(c)] = e[:, width:]
                aff[g, piece(c)] = a[:, :width]
                aff[h, piece(c)] = a[:, width:]
                mass = mass + fold_rows(e, jnp.sum)
                weighted = weighted + fold_rows(e * a, jnp.sum)
        if pair:
            mass = jnp.sum(mass, axis=0, keepdims=True)
            weighted = jnp.sum(weighted, axis=0, keepdims=True)
            for k, value in enumerate((peak, mass, weighted)):
                for n, (px, py) in enumerate(pair):
                    stat_own[px, k, py] = value[:, n * width : (n + 1) * width]
        return jnp.max(peak_n, axis=0, keepdims=True) if ahead else None

    def back_rows(out, px, py):
        g = px * NY + py
        pair = jnp.concatenate([weights[g], weights[g + 1]], axis=1)
        t = plain_dot(codes_t[...], pair).astype(BF)
        out[px, py] = t[:, :width]
        out[px, py + 1] = t[:, width:]

    def back_codes(part, at):
        where = pl.ds(pl.multiple_of(at, chunk), chunk)
        total = None
        for b in range(blocks):
            pair = jnp.concatenate([weights[2 * b, where], weights[2 * b + 1, where]], axis=1)
            term = plain_dot(pair, row_block(part, b // pairs, b % pairs * 2))
            total = term if total is None else total + term
        return total

    base = code * (2 * span) + low * span
    index = lax.broadcasted_iota(jnp.int32, (chunk, width), 0)

    def one_hot(b, carry):
        px, py = lax.div(b, pairs), lax.rem(b, pairs) * 2
        for side in range(2):
            local = tgt_all[px, py + side] - base
            for c in range(pieces):
                weights[2 * b + side, piece(c)] = jnp.where(index == local - c * chunk, 1.0, 0.0).astype(BF)
        back_rows(quant_out, px, py)
        return carry

    far_plane = (2, 1, 3, 0) if NX > 2 else (1, 0)
    side_c = channels // 2
    lower, upper = pl.ds(0, side_c), pl.ds(side_c, side_c)

    def send_plane(n, out, k):
        px = at_x(k)
        copies = []
        if k:
            copies.append(push(out.at[px, :, lower], rs_one.at[n, 0, x], rx_s.at[n, k], rx_r.at[n, k], to_x(k)))
        for j in range(1, NY):
            copies.append(
                push(out.at[px, at_y(j), upper], rs_one.at[n, 1, y, px], ry_s.at[n, k, j], ry_r.at[n, k, j], to_y(j))
            )
        return copies

    def reduce_one(n, out):
        for j in range(NY):
            total = out[x, j, lower].astype(F32)
            for k in range(1, NX):
                total = total + rs_one[n, 0, at_x(k), j].astype(F32)
            rs_mid[n, 0, j] = total.astype(BF)
        copies = [
            push(rs_mid.at[n, 0, at_y(k)], rs_two.at[n, 0, y], r2_s.at[n, 0, k], r2_r.at[n, 0, k], to_y(k))
            for k in range(1, NY)
        ]
        for j in range(NX):
            total = out[j, y, upper].astype(F32)
            for k in range(1, NY):
                total = total + rs_one[n, 1, at_y(k), j].astype(F32)
            rs_mid[n, 1, j] = total.astype(BF)
        return copies + [
            push(rs_mid.at[n, 1, at_x(k)], rs_two.at[n, 1, x], r2_s.at[n, 1, k], r2_r.at[n, 1, k], to_x(k))
            for k in range(1, NX)
        ]

    def reduce_two(n):
        left = rs_mid[n, 0, y].astype(F32)
        for k in range(1, NY):
            left = left + rs_two[n, 0, at_y(k)].astype(F32)
        right = rs_mid[n, 1, x].astype(F32)
        for k in range(1, NX):
            right = right + rs_two[n, 1, at_x(k)].astype(F32)
        total = jnp.concatenate([left, right], axis=0).T.astype(BF)
        rs_last[n] = total.reshape(NZ, own_rows, channels)
        return [
            push(rs_last.at[n, at_z(k)], rs_three.at[n, z], r3_s.at[n, k], r3_r.at[n, k], to_z(k))
            for k in far_first
        ]

    def reduce_three(n):
        total = rs_last[n, z].astype(F32)
        for k in range(1, NZ):
            total = total + rs_three[n, at_z(k)].astype(F32)
        return total

    def late(cell):
        rank = [k if k < 2 else NX - k + (NX if k == 2 else 0) for k in cell]
        return (min(cell) > 0) * max(rank), sum(rank)

    cells = sorted([(i, j) for i in range(NX) for j in range(NY)], key=late)
    here = set()

    def arrive_once(copy):
        if id(copy) not in here:
            here.add(id(copy))
            arrive([copy])

    pair, peak = None, None
    for n in range(0, groups + 2, 2):
        for i, j in cells[n : n + 2]:
            if i:
                arrive_once(lat_three[j, NX - i])
        for i, j in cells[n - 2 : n] if n else ():
            if j:
                arrive_once(up_three[i, NY - j])
        ahead = [(at_x(i), at_y(j)) for i, j in cells[n : n + 2]]
        peak = local_stats(pair, peak, ahead)
        pair = ahead
    arrive(tgt_three)

    sx = [push(stat_own.at[at_x(k)], stat_x.at[x], sx_s.at[k], sx_r.at[k], to_x(k)) for k in range(1, NX)]

    def picked(c, carry):
        at = c * chunk
        wide[pl.ds(pl.multiple_of(at, chunk), chunk)] = back_codes(1, at)
        return carry

    early = blocks * 5 // 8
    lax.fori_loop(0, early, one_hot, 0)
    arrive(sx)
    merged = merge_stats([stat_own[x]] + [stat_x[at_x(k)] for k in range(1, NX)])
    for k in range(3):
        stat_mid[0, k] = merged[k]
    sy = [push(stat_mid.at[0], stat_y.at[y], sy_s.at[k], sy_r.at[k], to_y(k)) for k in range(1, NY)]
    lax.fori_loop(early, blocks, one_hot, 0)
    arrive(sy)
    merged = merge_stats([merged] + [stat_y[at_y(k)] for k in range(1, NY)])
    for k in range(3):
        stat_mid[1, k] = merged[k]
    sz = [push(stat_mid.at[1], stat_z.at[z], sz_s.at[k], sz_r.at[k], to_z(k)) for k in far_first]
    quant_one = []
    for k in far_plane:
        quant_one += send_plane(1, quant_out, k)
    lax.fori_loop(0, pieces, picked, 0)
    arrive(sz)
    peak, mass, weighted = merge_stats([merged] + [stat_z[at_z(k)] for k in range(1, NZ)])
    for k, value in enumerate((peak, logit_scale / mass, weighted / mass)):
        stat_fin[x, k] = value
    sf = [push(stat_fin.at[x], stat_fin.at[x], sf_s.at[k], sf_r.at[k], to_x(k)) for k in range(1, NX)]

    def weigh(px):
        def body(j, carry):
            py = j * 2
            g = px * NY + py
            fade, mean = [], []
            for side in range(2):
                fade.append(
                    jnp.exp2((stat_own[px, 0, py + side] - stat_fin[px, 0, py + side]) * SCALE)
                    * stat_fin[px, 1, py + side]
                )
                mean.append(stat_fin[px, 2, py + side])
            total = None
            for c in range(0, pieces, 2):
                pair = []
                for side in range(2):
                    parts = []
                    for d in range(c, c + 2):
                        w = expo[g + side, piece(d)] * fade[side] * (aff[g + side, piece(d)] - mean[side])
                        weights[g + side, piece(d)] = w.astype(BF)
                        parts.append(w.astype(BF))
                    pair.append(jnp.concatenate(parts, axis=0))
                term = plain_dot(codes_t[:, c * chunk : (c + 2) * chunk], jnp.concatenate(pair, axis=1))
                total = term if total is None else total + term
            total = total.astype(BF)
            soft_out[px, py] = total[:, :width]
            soft_out[px, py + 1] = total[:, width:]
            return carry

        lax.fori_loop(0, pairs, body, 0)

    weigh(x)
    arrive(sf)
    soft_one = send_plane(0, soft_out, 0)
    for k in far_plane[:-1]:
        weigh(at_x(k))
        soft_one += send_plane(0, soft_out, k)
    arrive(quant_one)
    quant_two = reduce_one(1, quant_out)

    def grad_other(c, carry):
        at = (1 - core) * half + c * chunk
        where = pl.ds(pl.multiple_of(at, chunk), chunk)
        code_out[pl.ds(pl.multiple_of(c * chunk, chunk), chunk)] = (back_codes(0, at) + wide[where]).astype(BF)
        return carry

    lax.fori_loop(0, half // chunk, grad_other, 0)
    swap = push(code_out, code_in, core_s, core_r, twin)
    arrive(soft_one)
    soft_two = reduce_one(0, soft_out)

    def grad_own(c, carry):
        at = core * half + c * chunk
        where = pl.ds(pl.multiple_of(at, chunk), chunk)
        own_grad[pl.ds(pl.multiple_of(c * chunk, chunk), chunk)] = back_codes(0, at) + wide[where]
        return carry

    lax.fori_loop(0, half // chunk, grad_own, 0)
    arrive(quant_two)
    quant_three = reduce_two(1)
    arrive(soft_two)
    soft_three = reduce_two(0)
    for copy in adam_in:
        copy.wait()
    swap.wait_recv()

    def update(c, carry):
        where = pl.ds(pl.multiple_of(c * chunk, chunk), chunk)
        slope = own_grad[where] + code_in[where].astype(F32)
        fresh_one = beta_one * adam[1, where] + (1.0 - beta_one) * slope
        fresh_two = beta_two * adam[2, where] + (1.0 - beta_two) * slope * slope
        adam[1, where] = fresh_one
        adam[2, where] = fresh_two
        adam[0, where] = adam[0, where] - learn_rate * (fresh_one / (1.0 - beta_one**ADAM_2)) / (
            jnp.sqrt(fresh_two / (1.0 - beta_two**ADAM_2)) + adam_eps
        )
        return carry

    lax.fori_loop(0, half // chunk, update, 0)
    arrive(quant_three)
    terms_ref[1] = reduce_three(1)
    arrive(soft_three)
    terms_ref[0] = reduce_three(0)
    for copy in sent:
        copy.wait_send()


def exchange(latents, upstream, targets, codebook, moment_one, moment_two):
    own_rows, channels = latents.shape
    width = own_rows * NZ
    span = codebook.shape[0] // 2
    half = span // 2
    groups = NX * NY
    chunk = min(256, half)
    dma = pltpu.SemaphoreType.DMA
    side_c = channels // 2
    in_vmem = pl.BlockSpec(memory_space=pltpu.VMEM)
    anywhere = pl.BlockSpec(memory_space=pl.ANY)
    scratch = [
        pltpu.VMEM((2, NX, NY, NZ, own_rows, channels), BF),
        pltpu.VMEM((NZ, 1, width), jnp.int32),
        pltpu.VMEM((NX, NY, 1, width), jnp.int32),
        pltpu.VMEM((span, channels), F32),
        pltpu.VMEM((span, channels), BF),
        pltpu.VMEM((channels, span), BF),
        pltpu.VMEM((groups, span, width), F32),
        pltpu.VMEM((groups, span, width), F32),
        pltpu.VMEM((groups, span, width), BF),
        pltpu.VMEM((NX, NY, channels, width), BF),
        pltpu.VMEM((NX, NY, channels, width), BF),
        pltpu.VMEM((2, 2, NX, NY, side_c, width), BF),
        pltpu.VMEM((2, 2, NX, side_c, width), BF),
        pltpu.VMEM((2, 2, NX, side_c, width), BF),
        pltpu.VMEM((2, NZ, own_rows, channels), BF),
        pltpu.VMEM((2, NZ, own_rows, channels), BF),
        pltpu.VMEM((NX, 3, NY, 1, width), F32),
        pltpu.VMEM((NX, 3, NY, 1, width), F32),
        pltpu.VMEM((NY, 3, NY, 1, width), F32),
        pltpu.VMEM((NZ, 3, NY, 1, width), F32),
        pltpu.VMEM((2, 3, NY, 1, width), F32),
        pltpu.VMEM((NX, 3, NY, 1, width), F32),
        pltpu.VMEM((half, channels), BF),
        pltpu.VMEM((half, channels), BF),
        pltpu.VMEM((half, channels), F32),
        dma, dma((3,)),
        dma((NZ,)), dma((NZ,)), dma((2, NX)), dma((2, NX)), dma((2, NX, NX)), dma((2, NX, NX)),
        dma((NZ,)), dma((NZ,)), dma((NY,)), dma((NY,)), dma((NX,)), dma((NX,)),
        dma((NX,)), dma((NX,)), dma((NY,)), dma((NY,)), dma((NZ,)), dma((NZ,)), dma((NX,)), dma((NX,)),
        dma((2, NX)), dma((2, NX)), dma((2, NX, NY)), dma((2, NX, NY)),
        dma((2, 2, NX)), dma((2, 2, NX)), dma((2, NZ)), dma((2, NZ)),
        dma, dma,
    ]
    return pl.pallas_call(
        functools.partial(kernel, chunk),
        out_shape=(
            pltpu.VMEM((2, own_rows, channels), F32),
            pltpu.VMEM((3, half, channels), F32),
        ),
        in_specs=[in_vmem, in_vmem, pl.BlockSpec(memory_space=pltpu.SMEM), anywhere, anywhere, anywhere],
        out_specs=(in_vmem, in_vmem),
        scratch_shapes=scratch,
        compiler_params=pltpu.CompilerParams(
            collective_id=0, has_side_effects=True, vmem_limit_bytes=57 * 1024 * 1024
        ),
    )(latents, upstream, targets, codebook, moment_one, moment_two)


def finish(terms, lat, fresh, quant_ref, lat_ref, book_ref, one_ref, two_ref, sems):
    size = fresh.shape[1] // 4
    copies = [
        pltpu.make_async_copy(
            fresh.at[n, pl.ds(c * size, size)], target.at[0, pl.ds(c * size, size)], sems.at[n, c]
        )
        for c in range(4)
        for n, target in enumerate((book_ref, one_ref, two_ref))
    ]
    for copy in copies:
        copy.start()
    quant = terms[1]
    quant_ref[...] = quant.astype(BF)
    lat_ref[...] = terms[0] + commit_weight * (lat[...].astype(F32) - quant)
    for copy in copies:
        copy.wait()


def per_device(latents, upstream, targets, codebook, moment_one, moment_two):
    terms, fresh = exchange(latents, upstream, targets, codebook, moment_one, moment_two)
    in_vmem = pl.BlockSpec(memory_space=pltpu.VMEM)
    anywhere = pl.BlockSpec(memory_space=pl.ANY)
    moment = jax.ShapeDtypeStruct(moment_one.shape, F32)
    return pl.pallas_call(
        finish,
        out_shape=(
            jax.ShapeDtypeStruct(latents.shape, BF),
            jax.ShapeDtypeStruct(latents.shape, F32),
            moment, moment, moment,
        ),
        in_specs=[in_vmem, in_vmem, in_vmem],
        out_specs=(in_vmem, in_vmem, anywhere, anywhere, anywhere),
        scratch_shapes=[pltpu.SemaphoreType.DMA((3, 4))],
        compiler_params=pltpu.CompilerParams(vmem_limit_bytes=8 * 1024 * 1024),
    )(terms, latents, fresh)


def solution(mesh):
    return jax.shard_map(
        per_device,
        mesh=mesh,
        in_specs=(
            P(("dp", "code"), None),
            P(("dp", "code"), None),
            P(("dp", "code")),
            P("code", None),
            P("code", "dp", None),
            P("code", "dp", None),
        ),
        out_specs=(
            P(("dp", "code"), None),
            P(("dp", "code"), None),
            P("code", "dp", None),
            P("code", "dp", None),
            P("code", "dp", None),
        ),
        check_vma=False,
    )
```
